768 devices in a mesh: space: 192 (over z, y, core), group: 4 (over x).
Axes of the slice: x: 4, y: 8, z: 12, core: 2. Of those that a mesh axis runs over, the one named last changes fastest.
Arguments:
- snapshots: float32 [786432, 128], P(('space', 'group')), may hold values from -1500 to 1500
- last_snapshot: float32 [786432], P(('space', 'group')), may hold values from -1500 to 1500
Outputs:
- reduced_operator: float32 [128, 128], replicated
- mode_shapes: float32 [786432, 128], P(('space', 'group'))
The draws below stay inside these ranges and needn't reach their ends.
All inputs are finite; a program needn't handle non-finite values.
Results may differ from the reference program's by a relative error of at most 0.000068.
Values sent between devices are 32-bit elements; how exact they have to be, the bound alone decides.
No kernel may reach another device: no remote copies, remote signals or barrier semaphores. Data moves between devices by JAX's collectives and lax.ppermute only.
A program may use at most 32 MiB of HBM per device.

```python
import math
import jax
import jax.numpy as jnp
from jax import lax

K = 128
ROWS = 786432


def row_scales(key):
    salted = jax.random.fold_in(key, 7)
    spread = jax.random.uniform(salted, (ROWS,), jnp.float32)
    ramp = 1.0 + 2.0 * jnp.arange(ROWS, dtype=jnp.float32) / ROWS
    return ramp * jnp.exp(spread * math.log(10.0))


def draw_snapshots(key, part):
    salted = jax.random.fold_in(key, 11)
    column_scale = jnp.exp(jax.random.uniform(jax.random.fold_in(key, 13), (K,), jnp.float32) * math.log(10.0))
    values = jnp.clip(jax.random.normal(salted, (ROWS, K), jnp.float32), -5.0, 5.0)
    return (values * column_scale[None, :] * row_scales(key)[:, None]).astype(jnp.float32)


def draw_last_snapshot(key, part):
    salted = jax.random.fold_in(key, 23)
    column_scale = jnp.exp(jax.random.uniform(jax.random.fold_in(key, 29), (), jnp.float32) * math.log(10.0))
    values = jnp.clip(jax.random.normal(salted, (ROWS,), jnp.float32), -5.0, 5.0)
    return (values * column_scale * row_scales(key)).astype(jnp.float32)


def setup_inputs(seed: int = 0) -> dict:
    splits = jax.random.split(jax.random.key(seed), 3)
    snapshots = draw_snapshots(jax.random.fold_in(splits[2], 71), 0)
    last_snapshot = draw_last_snapshot(jax.random.fold_in(splits[2], 71), 0)
    return dict(snapshots=snapshots, last_snapshot=last_snapshot)


def transpose_product(left, right):
    return lax.dot_general(left.astype(jnp.float32), right.astype(jnp.float32), (((0,), (0,)), ((), ())), precision=lax.Precision.HIGHEST, preferred_element_type=jnp.float32)

def reference(snapshots, last_snapshot):
    highest = lax.Precision.HIGHEST
    second = jnp.concatenate([snapshots[:, 1:], last_snapshot[:, None]], axis=1)
    moment_one = transpose_product(snapshots, snapshots)
    moment_cross = transpose_product(snapshots, second)
    factor = jnp.linalg.cholesky(moment_one)
    identity = jnp.eye(moment_one.shape[0], dtype=jnp.float32)
    inverse = lax.linalg.triangular_solve(factor, identity, left_side=True, lower=True).T
    middle = jnp.dot(moment_cross.astype(jnp.float32), inverse.astype(jnp.float32), precision=highest, preferred_element_type=jnp.float32)
    reduced = jnp.dot(inverse.T.astype(jnp.float32), middle.astype(jnp.float32), precision=highest, preferred_element_type=jnp.float32)
    projected = jnp.dot(second.astype(jnp.float32), inverse.astype(jnp.float32), precision=highest, preferred_element_type=jnp.float32)
    mean_square = lax.optimization_barrier(jnp.mean(projected * projected, axis=0))
    mode_shapes = projected / jnp.sqrt(mean_square + 1e-06)[None, :]
    return (reduced, mode_shapes)
```

```python
import jax
import jax.numpy as jnp
from jax import lax
from jax.sharding import Mesh
from jax.sharding import PartitionSpec as P

HIGHEST = lax.Precision.HIGHEST
AXES = ("z", "y", "c", "x")
NEAR = ("y", "c")
FAR = ("z", "x")


def count(axes):
    total = 1
    for axis in axes:
        total *= lax.axis_size(axis)
    return total


def scatter_sum(table, axes):
    n = count(axes)
    blocks = table.reshape(n, table.shape[0] // n, table.shape[1])
    return lax.all_to_all(blocks, axes, 0, 0, tiled=True).sum(axis=0)


def exchange(block, axes):
    n = count(axes)
    copies = jnp.broadcast_to(block[None], (n, *block.shape))
    return lax.all_to_all(copies, axes, 0, 0, tiled=True)


def total_moments(table):
    block = scatter_sum(table, NEAR)
    block = exchange(block, FAR).sum(axis=0)
    return exchange(block, NEAR).reshape(table.shape)


def dot(left, right, dims):
    return lax.dot_general(
        left, right, (dims, ((), ())), precision=HIGHEST, preferred_element_type=jnp.float32
    )


def shards(snapshots, last_snapshot):
    k = snapshots.shape[1]
    row_count = snapshots.shape[0] * count(AXES)
    cross = dot(last_snapshot[None], snapshots, ((1,), (0,)))
    square = jnp.sum(last_snapshot * last_snapshot)
    corner = jnp.zeros((15, k), jnp.float32).at[0, 0].set(square)
    table = jnp.concatenate([dot(snapshots, snapshots, ((0,), (0,))), cross, corner])
    table = total_moments(table)
    moment_one, cross, square = table[:k], table[k], table[k + 1, 0]

    factor = jnp.linalg.cholesky(moment_one)
    identity = jnp.eye(k, dtype=jnp.float32)
    inverse = lax.linalg.triangular_solve(factor, identity, left_side=True, lower=True).T
    along = dot(inverse, cross, ((0,), (0,)))
    turned = jnp.concatenate([factor.T[:, 1:], along[:, None]], axis=1)
    reduced = dot(turned, inverse, ((1,), (0,)))
    outside = jnp.maximum(square - jnp.sum(along * along), 0.0)
    column_sums = jnp.sum(reduced * reduced, axis=0) + outside * inverse[k - 1] ** 2
    mean_square = column_sums / row_count
    second = jnp.concatenate([snapshots[:, 1:], last_snapshot[:, None]], axis=1)
    scaled = inverse / jnp.sqrt(mean_square + 1e-06)[None, :]
    return reduced, dot(second, scaled, ((1,), (0,)))


def solution(mesh):
    sizes = (12, 8, 2, 4)
    fine = Mesh(mesh.devices.reshape(sizes), AXES)
    in_specs = (P(AXES, None), P(AXES))
    out_specs = (P(), P(AXES, None))
    return jax.shard_map(shards, mesh=fine, in_specs=in_specs, out_specs=out_specs, check_vma=False)
```

```python
import functools

import jax
import jax.numpy as jnp
from jax import lax
from jax.experimental import pallas as pl
from jax.experimental.pallas import tpu as pltpu
from jax.sharding import Mesh
from jax.sharding import PartitionSpec as P

HIGHEST = lax.Precision.HIGHEST
B = 8


def dot(left, right, dims):
    return lax.dot_general(
        left, right, (dims, ((), ())), precision=HIGHEST, preferred_element_type=jnp.float32
    )


def moments_kernel(s_ref, last_ref, table_ref, turn_ref):
    rows, k = s_ref.shape
    lane = lax.broadcasted_iota(jnp.int32, (k, k), 1)
    row = lax.broadcasted_iota(jnp.int32, (k, k), 0)
    last = last_ref[...]
    columns = last.T
    total = jnp.zeros((k, k), jnp.float32)
    first = jnp.zeros((8, k), jnp.float32)
    for b in range(rows // k):
        part = s_ref[b * k : (b + 1) * k, :]
        turned = jnp.where(lane == 0, columns[:, b : b + 1], part)
        turn_ref[b * k : (b + 1) * k, :] = turned
        total += dot(part, turned, ((0,), (0,)))
        first += jnp.sum((part * part).reshape(k // 8, 8, k), axis=0)
    first = jnp.sum(first, axis=0, keepdims=True)[:, :1]
    square = jnp.sum(jnp.sum(last * last, axis=0, keepdims=True), axis=1, keepdims=True)
    total = jnp.where((row == k - 1) & (lane == 1), first, total)
    total = jnp.where((row == k - 1) & (lane == 2), square, total)
    table_ref[...] = total


def moments(s, last):
    rows, k = s.shape
    return pl.pallas_call(
        moments_kernel,
        out_shape=(
            jax.ShapeDtypeStruct((k, k), jnp.float32),
            jax.ShapeDtypeStruct((rows, k), jnp.float32),
        ),
        name="moments",
    )(s, last.reshape(rows // k, k))


def inverse_rows(w, k):
    lane = lax.broadcasted_iota(jnp.int32, (B, k), 1)
    sub = lax.broadcasted_iota(jnp.int32, (B, k), 0)
    shape = (B, k)
    out = []
    w = list(w)
    for g in range(k // B):
        at = g * B
        inside = (lane >= at) & (lane < at + B)
        raw = [jnp.broadcast_to(w[g][i : i + 1, :], shape) for i in range(B)]
        e = {}
        for i in range(B):
            for j in range(i, B):
                e[i, j] = jnp.broadcast_to(raw[i][:, at + j : at + j + 1], shape)
        p = [jnp.where(inside, (lane == at + i).astype(jnp.float32), raw[i]) for i in range(B)]
        rinv, low = [], {}
        rows = None
        for j in range(B):
            root = lax.rsqrt(e[j, j])
            r = root * root
            rinv.append(r)
            y = p[j] * root
            rows = y if rows is None else jnp.where(sub == j, y, rows)
            for i in range(j + 1, B):
                low[i, j] = e[j, i] * r
            for i in range(j + 1, B):
                for m in range(i, B):
                    e[i, m] = e[i, m] - low[i, j] * e[j, m]
                p[i] = p[i] - low[i, j] * p[j]
        out.append(rows)
        if g == k // B - 1:
            break
        q = [p[j] * rinv[j] for j in range(B)]
        for j in range(B - 1, 0, -1):
            for i in range(j):
                q[i] = q[i] - low[j, i] * q[j]
        for h in range(g + 1, k // B):
            s = [jnp.broadcast_to(w[h][:, at + j : at + j + 1], shape) for j in range(B)]
            t = [s[j] * q[j] for j in range(B)]
            while len(t) > 1:
                t = [t[n] + t[n + 1] for n in range(0, len(t), 2)]
            w[h] = jnp.where(inside, 0.0, w[h]) - t[0]
    return out


def modes_kernel(row_count, table_ref, turn_ref, reduced_ref, modes_ref):
    k = table_ref.shape[1]
    lane = lax.broadcasted_iota(jnp.int32, (k, k), 1)
    row = lax.broadcasted_iota(jnp.int32, (k, k), 0)
    table = table_ref[...]
    full = jnp.where(row <= lane, table, table.T)
    full = jnp.where((row == 0) & (lane == 0), table[k - 1 : k, 1:2], full)
    square = table[k - 1 : k, 2:3]
    cross = jnp.where(lane == 0, table, full)
    groups = inverse_rows([full[n : n + B] for n in range(0, k, B)], k)
    inv_t = jnp.where(row >= lane, jnp.concatenate(groups, axis=0), 0.0)
    turned_inv = pltpu.roll(inv_t, 1, 1)
    left = dot(inv_t, cross, ((1,), (0,)))
    reduced = dot(left, turned_inv, ((1,), (1,)))
    reduced_ref[...] = reduced
    along = jnp.sum(left * left, axis=0, keepdims=True)[:, :1]
    corner = inv_t[k - 1 : k, :]
    outside = jnp.maximum(square - along, 0.0)
    lane_row = lax.broadcasted_iota(jnp.int32, (1, k), 1)
    sums = jnp.sum(reduced * reduced, axis=0, keepdims=True)
    sums = sums + jnp.where(lane_row == k - 1, outside * corner * corner, 0.0)
    scale = lax.rsqrt(sums / row_count + 1e-06)
    modes_ref[...] = dot(turn_ref[...], turned_inv, ((1,), (1,))) * scale


def modes(row_count, table, turn):
    k = table.shape[1]
    return pl.pallas_call(
        functools.partial(modes_kernel, row_count),
        out_shape=(
            jax.ShapeDtypeStruct((k, k), jnp.float32),
            jax.ShapeDtypeStruct(turn.shape, jnp.float32),
        ),
        name="modes",
    )(table, turn)


AXES = ("z", "y", "c", "x")
NEAR = ("y", "c")
FAR = ("z", "x")


def count(axes):
    total = 1
    for axis in axes:
        total *= lax.axis_size(axis)
    return total


def scatter_sum(table, axes):
    n = count(axes)
    blocks = table.reshape(n, table.shape[0] // n, table.shape[1])
    return lax.all_to_all(blocks, axes, 0, 0, tiled=True).sum(axis=0)


def exchange(block, axes):
    n = count(axes)
    copies = jnp.broadcast_to(block[None], (n, *block.shape))
    return lax.all_to_all(copies, axes, 0, 0, tiled=True)


def total_moments(table):
    block = scatter_sum(table, NEAR)
    block = exchange(block, FAR).sum(axis=0)
    return exchange(block, NEAR).reshape(table.shape)


def shards(snapshots, last_snapshot):
    row_count = snapshots.shape[0] * count(AXES)
    table, turn = moments(snapshots, last_snapshot)
    return modes(row_count, total_moments(table), turn)


def solution(mesh):
    sizes = (12, 8, 2, 4)
    fine = Mesh(mesh.devices.reshape(sizes), AXES)
    in_specs = (P(AXES, None), P(AXES))
    out_specs = (P(), P(AXES, None))
    return jax.shard_map(shards, mesh=fine, in_specs=in_specs, out_specs=out_specs, check_vma=False)
```

```python
import functools

import jax
import jax.numpy as jnp
from jax import lax
from jax.experimental import pallas as pl
from jax.experimental.pallas import tpu as pltpu
from jax.sharding import Mesh
from jax.sharding import PartitionSpec as P

HIGHEST = lax.Precision.HIGHEST
B = 8
VMEM_BYTES = 16 * 2**20


def dot(left, right, dims):
    return lax.dot_general(
        left, right, (dims, ((), ())), precision=HIGHEST, preferred_element_type=jnp.float32
    )


def split(x):
    high = x.astype(jnp.bfloat16)
    rest = x - high.astype(jnp.float32)
    middle = rest.astype(jnp.bfloat16)
    return high, middle, (rest - middle.astype(jnp.float32)).astype(jnp.bfloat16)


def product(left, right):
    return lax.dot_general(
        left, right, (((1,), (0,)), ((), ())), preferred_element_type=jnp.float32
    )


def gram(s, last):
    rows, k = s.shape
    sub = lax.broadcasted_iota(jnp.int32, (16, k), 0)
    spread = jnp.concatenate([last, jnp.zeros_like(last)], axis=0)
    spread = jnp.concatenate([jnp.where(sub == b, spread, 0.0) for b in range(rows // k)], axis=1)
    high, middle, low = split(s)
    last_high, last_middle, last_low = split(spread)
    lead = jnp.concatenate([high.T, last_high], axis=0)
    first = product(lead, jnp.concatenate([high, middle], axis=1))
    second = product(lead, low)
    third = product(jnp.concatenate([middle.T, last_middle], axis=0), middle)
    fourth = product(jnp.concatenate([last_middle, last_low], axis=0), high)
    mixed = first[:k, k:] + second[:k]
    square = (mixed + mixed.T) + third[:k] + first[:k, :k]
    cross = fourth[16:] + second[k:] + third[k:] + first[k:, k:] + fourth[:16] + first[k:, :k]
    return square, jnp.sum(cross, axis=0, keepdims=True)


def moments_kernel(s_ref, last_ref, table_ref):
    k = s_ref.shape[1]
    last = last_ref[...]
    square, along = gram(s_ref[...], last)
    norm = jnp.sum(jnp.sum(last * last, axis=0, keepdims=True), axis=1, keepdims=True)
    sub = lax.broadcasted_iota(jnp.int32, (8, k), 0)
    lane = lax.broadcasted_iota(jnp.int32, (8, k), 1)
    tail = jnp.where((sub == 7) & (lane < k - 1), along, square[k - 8 :])
    tail = jnp.where((sub == 6) & (lane == 0), along[:, k - 1 :], tail)
    table_ref[0 : k - 8, :] = square[: k - 8]
    table_ref[k - 8 :, :] = jnp.where((sub == 6) & (lane == 1), norm, tail)


def moments(s, last):
    rows, k = s.shape
    return pl.pallas_call(
        moments_kernel,
        out_shape=jax.ShapeDtypeStruct((k, k), jnp.float32),
        name="moments",
    )(s, last.reshape(rows // k, k))


def turn_kernel(s_ref, last_ref, turn_ref):
    rows, k = s_ref.shape
    lane = lax.broadcasted_iota(jnp.int32, (k, k), 1)
    columns = last_ref[...].T
    for b in range(rows // k):
        part = s_ref[b * k : (b + 1) * k, :]
        turn_ref[b * k : (b + 1) * k, :] = jnp.where(lane == 0, columns[:, b : b + 1], part)


def turn_columns(s, last):
    rows, k = s.shape
    return pl.pallas_call(
        turn_kernel,
        out_shape=jax.ShapeDtypeStruct((rows, k), jnp.float32),
        compiler_params=pltpu.CompilerParams(vmem_limit_bytes=VMEM_BYTES),
        cost_estimate=pl.CostEstimate(flops=rows * k, bytes_accessed=8 * rows * k, transcendentals=0),
        name="turn_columns",
    )(s, last.reshape(rows // k, k))


def inverse_rows(w, k):
    lane = lax.broadcasted_iota(jnp.int32, (B, k), 1)
    sub = lax.broadcasted_iota(jnp.int32, (B, k), 0)

    def wide(column):
        return jnp.broadcast_to(column, (B, k))

    out, w = [], list(w)
    groups = k // B
    for g in range(groups):
        at = g * B
        inside = (lane >= at) & (lane < at + B)
        columns = [wide(w[g][:, at + j : at + j + 1]) for j in range(B)]
        e = {(i, j): wide(columns[j][i : i + 1, :]) for j in range(B) for i in range(j + 1)}
        p = [
            jnp.where(inside, (lane == at + i).astype(jnp.float32), wide(w[g][i : i + 1, :]))
            for i in range(B)
        ]
        inner = g < groups - 1
        if inner:
            s = [wide(w[g + 1][:, at + j : at + j + 1]) for j in range(B)]
            after = jnp.where(inside, 0.0, w[g + 1])
        low, inv, pivot = {}, [None] * B, [None] * B
        for j in range(0, B, 2):
            n = j + 1
            a, b, c = e[j, j], e[j, n], e[n, n]
            ra, rd = 1.0 / a, 1.0 / (a * c - b * b)
            rs = a * rd
            inv[j], inv[n] = ra, rs
            for i in range(n, B):
                low[i, j] = e[j, i] * ra
            for m in range(j + 2, B):
                e[n, m] = e[n, m] - low[n, j] * e[j, m]
                low[m, n] = e[n, m] * rs
            pivot[j], pivot[n] = a, c - low[n, j] * b
            p[n] = p[n] - low[n, j] * p[j]
            for i in range(j + 2, B):
                for m in range(i, B):
                    e[i, m] = (e[i, m] - low[i, j] * e[j, m]) - low[i, n] * e[n, m]
                p[i] = (p[i] - low[i, j] * p[j]) - low[i, n] * p[n]
            if inner:
                s[n] = s[n] - s[j] * low[n, j]
                for m in range(j + 2, B):
                    s[m] = (s[m] - s[j] * low[m, j]) - s[n] * low[m, n]
                after = after - (s[j] * (p[j] * ra) + s[n] * (p[n] * rs))
        rows = None
        for j in range(B):
            y = p[j] * lax.rsqrt(pivot[j])
            rows = y if rows is None else jnp.where(sub == j, y, rows)
        out.append(rows)
        if not inner:
            break
        w[g + 1] = after
        if g + 2 == groups:
            continue
        q = [p[j] * inv[j] for j in range(B)]
        for j in range(B - 1, 0, -1):
            for i in range(j):
                q[i] = q[i] - low[j, i] * q[j]
        for h in range(g + 2, groups):
            t = [wide(w[h][:, at + j : at + j + 1]) * q[j] for j in range(B)]
            while len(t) > 1:
                t = [t[n] + t[n + 1] for n in range(0, len(t), 2)]
            w[h] = jnp.where(inside, 0.0, w[h]) - t[0]
    return out


def modes_kernel(row_count, chunks, table_ref, turn_ref, reduced_hbm, modes_hbm, full_modes, small, sems):
    k = table_ref.shape[1]
    lane = lax.broadcasted_iota(jnp.int32, (k, k), 1)
    row = lax.broadcasted_iota(jnp.int32, (k, k), 0)
    table = table_ref[...]
    flip = table.T
    full = jnp.where(row <= lane, table, flip)
    last = jnp.where(row == k - 1, table[k - 2 : k - 1, 0:1], flip[:, k - 1 : k])
    square = table[k - 2 : k - 1, 1:2]
    cross = jnp.where(lane == 0, last, full)
    diagonal = jnp.where(row == lane, full, 0.0)
    across = lax.rsqrt(jnp.sum(diagonal, axis=0, keepdims=True))
    down = lax.rsqrt(jnp.sum(diagonal, axis=1, keepdims=True))
    unit = full * across * down
    groups = inverse_rows([unit[n : n + B] for n in range(0, k, B)], k)
    inv_t = jnp.where(row >= lane, jnp.concatenate(groups, axis=0), 0.0) * across
    turned_inv = pltpu.roll(inv_t, 1, 1)
    left = dot(inv_t, cross, ((1,), (0,)))
    full_modes[...] = dot(turn_ref[...], turned_inv, ((1,), (1,)))
    reduced = dot(left, turned_inv, ((1,), (1,)))
    small[...] = reduced
    copies = [pltpu.make_async_copy(small, reduced_hbm, sems.at[chunks])]
    copies[0].start()
    along = jnp.sum(left * left, axis=0, keepdims=True)[:, :1]
    corner = inv_t[k - 1 : k, :]
    outside = jnp.maximum(square - along, 0.0)
    lane_row = lax.broadcasted_iota(jnp.int32, (1, k), 1)
    sums = jnp.sum(reduced * reduced, axis=0, keepdims=True)
    sums = sums + jnp.where(lane_row == k - 1, outside * corner * corner, 0.0)
    scale = lax.rsqrt(sums / row_count + 1e-06)
    size = full_modes.shape[0] // chunks
    for n in range(chunks):
        part = pl.ds(n * size, size)
        full_modes[part, :] = full_modes[part, :] * scale
        copies.append(pltpu.make_async_copy(full_modes.at[part, :], modes_hbm.at[part, :], sems.at[n]))
        copies[-1].start()
    for copy in copies:
        copy.wait()


def modes(row_count, table, turn, chunks=4):
    k = table.shape[1]
    return pl.pallas_call(
        functools.partial(modes_kernel, row_count, chunks),
        out_shape=(
            jax.ShapeDtypeStruct((k, k), jnp.float32),
            jax.ShapeDtypeStruct(turn.shape, jnp.float32),
        ),
        in_specs=[pl.BlockSpec(memory_space=pltpu.VMEM)] * 2,
        out_specs=(pl.BlockSpec(memory_space=pl.ANY),) * 2,
        scratch_shapes=[
            pltpu.VMEM(turn.shape, jnp.float32),
            pltpu.VMEM((k, k), jnp.float32),
            pltpu.SemaphoreType.DMA((chunks + 1,)),
        ],
        compiler_params=pltpu.CompilerParams(vmem_limit_bytes=VMEM_BYTES),
        name="modes",
    )(table, turn)


AXES = ("z", "y", "c", "x")
NEAR = ("y", "c")
FAR = ("z", "x")


def count(axes):
    total = 1
    for axis in axes:
        total *= lax.axis_size(axis)
    return total


def scatter_sum(table, axes):
    n = count(axes)
    blocks = table.reshape(n, table.shape[0] // n, table.shape[1])
    return lax.all_to_all(blocks, axes, 0, 0, tiled=True).sum(axis=0)


def exchange(block, axes):
    n = count(axes)
    copies = jnp.broadcast_to(block[None], (n, *block.shape))
    return lax.all_to_all(copies, axes, 0, 0, tiled=True)


def total_moments(table):
    block = scatter_sum(table, NEAR)
    block = exchange(block, FAR).sum(axis=0)
    return exchange(block, NEAR).reshape(table.shape)


def shards(snapshots, last_snapshot):
    row_count = snapshots.shape[0] * count(AXES)
    table = moments(snapshots, last_snapshot)
    turn = turn_columns(snapshots, last_snapshot)
    return modes(row_count, total_moments(table), turn)


def solution(mesh):
    sizes = (12, 8, 2, 4)
    fine = Mesh(mesh.devices.reshape(sizes), AXES)
    in_specs = (P(AXES, None), P(AXES))
    out_specs = (P(), P(AXES, None))
    return jax.shard_map(shards, mesh=fine, in_specs=in_specs, out_specs=out_specs, check_vma=False)
```

```python
import functools

import jax
import jax.numpy as jnp
from jax import lax
from jax.experimental import pallas as pl
from jax.experimental.pallas import tpu as pltpu
from jax.sharding import Mesh
from jax.sharding import PartitionSpec as P

HIGHEST = lax.Precision.HIGHEST
B = 8
VMEM_BYTES = 62000000
TURN_AT = 8


def dot(left, right, dims):
    return lax.dot_general(
        left, right, (dims, ((), ())), precision=HIGHEST, preferred_element_type=jnp.float32
    )


def split(x):
    high = x.astype(jnp.bfloat16)
    rest = x - high.astype(jnp.float32)
    middle = rest.astype(jnp.bfloat16)
    return high, middle, (rest - middle.astype(jnp.float32)).astype(jnp.bfloat16)


def product(left, right):
    return lax.dot_general(
        left, right, (((1,), (0,)), ((), ())), preferred_element_type=jnp.float32
    )


def gram(s, last):
    rows, k = s.shape
    sub = lax.broadcasted_iota(jnp.int32, (16, k), 0)
    spread = jnp.concatenate([last, jnp.zeros_like(last)], axis=0)
    spread = jnp.concatenate([jnp.where(sub == b, spread, 0.0) for b in range(rows // k)], axis=1)
    high, middle, low = split(s)
    last_high, last_middle, last_low = split(spread)
    lead = jnp.concatenate([high.T, last_high], axis=0)
    first = product(lead, jnp.concatenate([high, middle], axis=1))
    second = product(lead, low)
    third = product(jnp.concatenate([middle.T, last_middle], axis=0), middle)
    fourth = product(jnp.concatenate([last_middle, last_low], axis=0), high)
    mixed = first[:k, k:] + second[:k]
    square = (mixed + mixed.T) + third[:k] + first[:k, :k]
    cross = fourth[16:] + second[k:] + third[k:] + first[k:, k:] + fourth[:16] + first[k:, :k]
    return square, jnp.sum(cross, axis=0, keepdims=True)


def moments_kernel(s_ref, last_ref, table_ref):
    k = s_ref.shape[1]
    h = k // 2
    last = last_ref[...]
    square, along = gram(s_ref[...], last)
    norm = jnp.sum(jnp.sum(last * last, axis=0, keepdims=True), axis=1, keepdims=True)
    row = lax.broadcasted_iota(jnp.int32, (h, k), 0)
    lane = lax.broadcasted_iota(jnp.int32, (h, k), 1)
    end = square[h:]
    table_ref[0:h, :] = jnp.where((lane < h) & (row > lane), pltpu.roll(end, h, 1), square[:h])
    diagonal = jnp.sum(jnp.where(row + h == lane, end, 0.0), axis=0, keepdims=True)
    diagonal = jnp.where(lane[:1] == 0, norm, diagonal)
    rest = table_ref.shape[0] - h
    sub = lax.broadcasted_iota(jnp.int32, (rest, k), 0)
    table_ref[h:, :] = jnp.where(sub == 0, along, jnp.where(sub == 1, diagonal, 0.0))


def moments(s, last, table_rows):
    rows, k = s.shape
    return pl.pallas_call(
        moments_kernel,
        out_shape=jax.ShapeDtypeStruct((table_rows, k), jnp.float32),
        name="moments",
    )(s, last.reshape(rows // k, k))


def inverse_rows(w, k, between):
    lane = lax.broadcasted_iota(jnp.int32, (B, k), 1)
    sub = lax.broadcasted_iota(jnp.int32, (B, k), 0)

    def wide(column):
        return jnp.broadcast_to(column, (B, k))

    out, w = [], list(w)
    groups = k // B
    for g in range(groups):
        if g in between:
            between[g]()
        at = g * B
        inside = (lane >= at) & (lane < at + B)
        columns = [wide(w[g][:, at + j : at + j + 1]) for j in range(B)]
        e = {(i, j): wide(columns[j][i : i + 1, :]) for j in range(B) for i in range(j + 1)}
        p = [
            jnp.where(inside, (lane == at + i).astype(jnp.float32), wide(w[g][i : i + 1, :]))
            for i in range(B)
        ]
        inner = g < groups - 1
        if inner:
            s = [wide(w[g + 1][:, at + j : at + j + 1]) for j in range(B)]
            after = jnp.where(inside, 0.0, w[g + 1])
        low, inv, pivot = {}, [None] * B, [None] * B
        for j in range(0, B, 2):
            n = j + 1
            a, b, c = e[j, j], e[j, n], e[n, n]
            ra, rd = 1.0 / a, 1.0 / (a * c - b * b)
            rs = a * rd
            inv[j], inv[n] = ra, rs
            for i in range(n, B):
                low[i, j] = e[j, i] * ra
            for m in range(j + 2, B):
                e[n, m] = e[n, m] - low[n, j] * e[j, m]
                low[m, n] = e[n, m] * rs
            pivot[j], pivot[n] = a, c - low[n, j] * b
            p[n] = p[n] - low[n, j] * p[j]
            for i in range(j + 2, B):
                for m in range(i, B):
                    e[i, m] = (e[i, m] - low[i, j] * e[j, m]) - low[i, n] * e[n, m]
                p[i] = (p[i] - low[i, j] * p[j]) - low[i, n] * p[n]
            if inner:
                s[n] = s[n] - s[j] * low[n, j]
                for m in range(j + 2, B):
                    s[m] = (s[m] - s[j] * low[m, j]) - s[n] * low[m, n]
                after = after - (s[j] * (p[j] * ra) + s[n] * (p[n] * rs))
        rows = None
        for j in range(B):
            y = p[j] * lax.rsqrt(pivot[j])
            rows = y if rows is None else jnp.where(sub == j, y, rows)
        out.append(rows)
        if not inner:
            break
        w[g + 1] = after
        if g + 2 == groups:
            continue
        q = [p[j] * inv[j] for j in range(B)]
        for j in range(B - 1, 0, -1):
            for i in range(j):
                q[i] = q[i] - low[j, i] * q[j]
        for h in range(g + 2, groups):
            t = [wide(w[h][:, at + j : at + j + 1]) * q[j] for j in range(B)]
            while len(t) > 1:
                t = [t[n] + t[n + 1] for n in range(0, len(t), 2)]
            w[h] = jnp.where(inside, 0.0, w[h]) - t[0]
    return out


def unfold(table):
    k = table.shape[1]
    h = k // 2
    row = lax.broadcasted_iota(jnp.int32, (h, k), 0)
    lane = lax.broadcasted_iota(jnp.int32, (h, k), 1)
    flip = jnp.concatenate([table, jnp.zeros((k - table.shape[0], k), jnp.float32)], axis=0).T
    head = table[:h]
    top = jnp.where((lane >= h) | (row <= lane), head, flip[:h])
    end = pltpu.roll(jnp.where(row > lane, head, flip[:h]), h, 1)
    end = jnp.where(row + h == lane, table[h + 1 : h + 2, :], end)
    bottom = jnp.where(lane < h, flip[h:], end)
    return jnp.concatenate([top, bottom], axis=0), flip[:, h : h + 1], table[h + 1 : h + 2, 0:1]


def modes_kernel(row_count, chunks, table_ref, s_hbm, last_hbm, reduced_hbm, modes_hbm, *scratch):
    turn_ref, last_ref, full_modes, small, sems, in_sems = scratch
    k = table_ref.shape[1]
    loads = [
        pltpu.make_async_copy(last_hbm, last_ref, in_sems.at[0]),
        pltpu.make_async_copy(s_hbm, turn_ref, in_sems.at[1]),
    ]
    for load in loads:
        load.start()
    lane = lax.broadcasted_iota(jnp.int32, (k, k), 1)
    row = lax.broadcasted_iota(jnp.int32, (k, k), 0)
    full, last, square = unfold(table_ref[...])
    cross = jnp.where(lane == 0, last, full)
    diagonal = jnp.where(row == lane, full, 0.0)
    across = lax.rsqrt(jnp.sum(diagonal, axis=0, keepdims=True))
    down = lax.rsqrt(jnp.sum(diagonal, axis=1, keepdims=True))
    unit = full * across * down

    def turn_columns():
        for load in loads:
            load.wait()
        columns = last_ref[...].T
        for b in range(turn_ref.shape[0] // k):
            part = slice(b * k, (b + 1) * k)
            turn_ref[part, :] = jnp.where(lane == 0, columns[:, b : b + 1], turn_ref[part, :])

    groups = inverse_rows([unit[n : n + B] for n in range(0, k, B)], k, {TURN_AT: turn_columns})
    inv_t = jnp.where(row >= lane, jnp.concatenate(groups, axis=0), 0.0) * across
    turned_inv = pltpu.roll(inv_t, 1, 1)
    left = dot(inv_t, cross, ((1,), (0,)))
    full_modes[...] = dot(turn_ref[...], turned_inv, ((1,), (1,)))
    reduced = dot(left, turned_inv, ((1,), (1,)))
    small[...] = reduced
    copies = [pltpu.make_async_copy(small, reduced_hbm, sems.at[chunks])]
    copies[0].start()
    along = jnp.sum(left * left, axis=0, keepdims=True)[:, :1]
    corner = inv_t[k - 1 : k, :]
    outside = jnp.maximum(square - along, 0.0)
    lane_row = lax.broadcasted_iota(jnp.int32, (1, k), 1)
    sums = jnp.sum(reduced * reduced, axis=0, keepdims=True)
    sums = sums + jnp.where(lane_row == k - 1, outside * corner * corner, 0.0)
    scale = lax.rsqrt(sums / row_count + 1e-06)
    size = full_modes.shape[0] // chunks
    for n in range(chunks):
        part = pl.ds(n * size, size)
        full_modes[part, :] = full_modes[part, :] * scale
        copies.append(pltpu.make_async_copy(full_modes.at[part, :], modes_hbm.at[part, :], sems.at[n]))
        copies[-1].start()
    for copy in copies:
        copy.wait()


def modes(row_count, table, s, last, chunks=4):
    rows, k = s.shape
    return pl.pallas_call(
        functools.partial(modes_kernel, row_count, chunks),
        out_shape=(
            jax.ShapeDtypeStruct((k, k), jnp.float32),
            jax.ShapeDtypeStruct(s.shape, jnp.float32),
        ),
        in_specs=[
            pl.BlockSpec(memory_space=pltpu.VMEM),
            pl.BlockSpec(memory_space=pl.ANY),
            pl.BlockSpec(memory_space=pl.ANY),
        ],
        out_specs=(pl.BlockSpec(memory_space=pl.ANY),) * 2,
        scratch_shapes=[
            pltpu.VMEM(s.shape, jnp.float32),
            pltpu.VMEM((rows // k, k), jnp.float32),
            pltpu.VMEM(s.shape, jnp.float32),
            pltpu.VMEM((k, k), jnp.float32),
            pltpu.SemaphoreType.DMA((chunks + 1,)),
            pltpu.SemaphoreType.DMA((2,)),
        ],
        compiler_params=pltpu.CompilerParams(vmem_limit_bytes=VMEM_BYTES),
        name="modes",
    )(table, s, last.reshape(rows // k, k))


AXES = ("z", "y", "c", "x")
NEAR = ("y", "c")
FAR = ("z", "x")
PIECE = 5


def count(axes):
    total = 1
    for axis in axes:
        total *= lax.axis_size(axis)
    return total


def exchange(block, axes):
    n = count(axes)
    copies = jnp.broadcast_to(block[None], (n, *block.shape))
    return lax.all_to_all(copies, axes, 0, 0, tiled=True)


def total_moments(table):
    n = count(NEAR)
    pieces = table.reshape(n, table.shape[0] // n, 1, table.shape[1])
    piece = lax.all_to_all(pieces, NEAR, 0, 0, tiled=True).sum(axis=0)
    piece = exchange(piece, FAR).sum(axis=0)
    return exchange(piece, NEAR).reshape(table.shape)


def shards(snapshots, last_snapshot):
    row_count = snapshots.shape[0] * count(AXES)
    table = moments(snapshots, last_snapshot, PIECE * count(NEAR))
    return modes(row_count, total_moments(table), snapshots, last_snapshot)


def solution(mesh):
    sizes = (12, 8, 2, 4)
    fine = Mesh(mesh.devices.reshape(sizes), AXES)
    in_specs = (P(AXES, None), P(AXES))
    out_specs = (P(), P(AXES, None))
    return jax.shard_map(shards, mesh=fine, in_specs=in_specs, out_specs=out_specs, check_vma=False)
```

```python
import functools

import jax
import jax.numpy as jnp
from jax import lax
from jax.experimental import pallas as pl
from jax.experimental.pallas import tpu as pltpu
from jax.sharding import Mesh
from jax.sharding import PartitionSpec as P

HIGHEST = lax.Precision.HIGHEST
B = 8
VMEM_BYTES = 62000000
TURN_AT = 8


def dot(left, right, dims):
    return lax.dot_general(
        left, right, (dims, ((), ())), precision=HIGHEST, preferred_element_type=jnp.float32
    )


def split(x):
    high = x.astype(jnp.bfloat16)
    rest = x - high.astype(jnp.float32)
    middle = rest.astype(jnp.bfloat16)
    return high, middle, (rest - middle.astype(jnp.float32)).astype(jnp.bfloat16)


def product(left, right):
    return lax.dot_general(
        left, right, (((1,), (0,)), ((), ())), preferred_element_type=jnp.float32
    )


def gram(s, last):
    rows, k = s.shape
    sub = lax.broadcasted_iota(jnp.int32, (16, k), 0)
    spread = jnp.concatenate([last, jnp.zeros_like(last)], axis=0)
    spread = jnp.concatenate([jnp.where(sub == b, spread, 0.0) for b in range(rows // k)], axis=1)
    high, middle, low = split(s)
    last_high, last_middle, last_low = split(spread)
    lead = jnp.concatenate([high.T, last_high], axis=0)
    first = product(lead, jnp.concatenate([high, middle], axis=1))
    second = product(lead, low)
    third = product(jnp.concatenate([middle.T, last_middle], axis=0), middle)
    fourth = product(jnp.concatenate([last_middle, last_low], axis=0), high)
    mixed = first[:k, k:] + second[:k]
    square = (mixed + mixed.T) + third[:k] + first[:k, :k]
    cross = fourth[16:] + second[k:] + third[k:] + first[k:, k:] + fourth[:16] + first[k:, :k]
    return square, jnp.sum(cross, axis=0, keepdims=True)


def moments_kernel(s_ref, last_ref, table_ref):
    k = s_ref.shape[1]
    h = k // 2
    last = last_ref[...]
    square, along = gram(s_ref[...], last)
    norm = jnp.sum(jnp.sum(last * last, axis=0, keepdims=True), axis=1, keepdims=True)
    row = lax.broadcasted_iota(jnp.int32, (h, k), 0)
    lane = lax.broadcasted_iota(jnp.int32, (h, k), 1)
    end = square[h:]
    table_ref[0:h, :] = jnp.where((lane < h) & (row > lane), pltpu.roll(end, h, 1), square[:h])
    diagonal = jnp.sum(jnp.where(row + h == lane, end, 0.0), axis=0, keepdims=True)
    diagonal = jnp.where(lane[:1] == 0, norm, diagonal)
    rest = table_ref.shape[0] - h
    sub = lax.broadcasted_iota(jnp.int32, (rest, k), 0)
    table_ref[h:, :] = jnp.where(sub == 0, along, jnp.where(sub == 1, diagonal, 0.0))


def moments(s, last, table_rows):
    rows, k = s.shape
    return pl.pallas_call(
        moments_kernel,
        out_shape=jax.ShapeDtypeStruct((table_rows, k), jnp.float32),
        name="moments",
    )(s, last.reshape(rows // k, k))


def inverse_rows(w, k, between):
    lane = lax.broadcasted_iota(jnp.int32, (B, k), 1)
    sub = lax.broadcasted_iota(jnp.int32, (B, k), 0)

    def wide(column):
        return jnp.broadcast_to(column, (B, k))

    out, w = [], list(w)
    groups = k // B
    for g in range(groups):
        if g in between:
            between[g]()
        at = g * B
        inside = (lane >= at) & (lane < at + B)
        columns = [wide(w[g][:, at + j : at + j + 1]) for j in range(B)]
        e = {(i, j): wide(columns[j][i : i + 1, :]) for j in range(B) for i in range(j + 1)}
        p = [
            jnp.where(inside, (lane == at + i).astype(jnp.float32), wide(w[g][i : i + 1, :]))
            for i in range(B)
        ]
        inner = g < groups - 1
        if inner:
            s = [wide(w[g + 1][:, at + j : at + j + 1]) for j in range(B)]
            after = jnp.where(inside, 0.0, w[g + 1])
        low, inv, pivot = {}, [None] * B, [None] * B
        for j in range(0, B, 2):
            n = j + 1
            a, b, c = e[j, j], e[j, n], e[n, n]
            ra, rd = 1.0 / a, 1.0 / (a * c - b * b)
            rs = a * rd
            inv[j], inv[n] = ra, rs
            for i in range(n, B):
                low[i, j] = e[j, i] * ra
            for m in range(j + 2, B):
                e[n, m] = e[n, m] - low[n, j] * e[j, m]
                low[m, n] = e[n, m] * rs
            pivot[j], pivot[n] = a, c - low[n, j] * b
            p[n] = p[n] - low[n, j] * p[j]
            for i in range(j + 2, B):
                for m in range(i, B):
                    e[i, m] = (e[i, m] - low[i, j] * e[j, m]) - low[i, n] * e[n, m]
                p[i] = (p[i] - low[i, j] * p[j]) - low[i, n] * p[n]
            if inner:
                s[n] = s[n] - s[j] * low[n, j]
                for m in range(j + 2, B):
                    s[m] = (s[m] - s[j] * low[m, j]) - s[n] * low[m, n]
                after = after - (s[j] * (p[j] * ra) + s[n] * (p[n] * rs))
        rows = None
        for j in range(B):
            y = p[j] * lax.rsqrt(pivot[j])
            rows = y if rows is None else jnp.where(sub == j, y, rows)
        out.append(rows)
        if not inner:
            break
        w[g + 1] = after
        if g + 2 == groups:
            continue
        q = [p[j] * inv[j] for j in range(B)]
        for j in range(B - 1, 0, -1):
            for i in range(j):
                q[i] = q[i] - low[j, i] * q[j]
        for h in range(g + 2, groups):
            t = [wide(w[h][:, at + j : at + j + 1]) * q[j] for j in range(B)]
            while len(t) > 1:
                t = [t[n] + t[n + 1] for n in range(0, len(t), 2)]
            w[h] = jnp.where(inside, 0.0, w[h]) - t[0]
    return out


def unfold(table):
    k = table.shape[1]
    h = k // 2
    row = lax.broadcasted_iota(jnp.int32, (h, k), 0)
    lane = lax.broadcasted_iota(jnp.int32, (h, k), 1)
    flip = jnp.concatenate([table, jnp.zeros((k - table.shape[0], k), jnp.float32)], axis=0).T
    head = table[:h]
    top = jnp.where((lane >= h) | (row <= lane), head, flip[:h])
    end = pltpu.roll(jnp.where(row > lane, head, flip[:h]), h, 1)
    end = jnp.where(row + h == lane, table[h + 1 : h + 2, :], end)
    bottom = jnp.where(lane < h, flip[h:], end)
    return jnp.concatenate([top, bottom], axis=0), flip[:, h : h + 1], table[h + 1 : h + 2, 0:1]


def modes_kernel(row_count, chunks, table_ref, s_hbm, last_hbm, reduced_hbm, modes_hbm, *scratch):
    turn_ref, last_ref, full_modes, small, sems, in_sems = scratch
    k = table_ref.shape[1]
    loads = [
        pltpu.make_async_copy(last_hbm, last_ref, in_sems.at[0]),
        pltpu.make_async_copy(s_hbm, turn_ref, in_sems.at[1]),
    ]
    for load in loads:
        load.start()
    lane = lax.broadcasted_iota(jnp.int32, (k, k), 1)
    row = lax.broadcasted_iota(jnp.int32, (k, k), 0)
    full, last, square = unfold(table_ref[...])
    cross = jnp.where(lane == 0, last, full)
    diagonal = jnp.where(row == lane, full, 0.0)
    across = lax.rsqrt(jnp.sum(diagonal, axis=0, keepdims=True))
    down = lax.rsqrt(jnp.sum(diagonal, axis=1, keepdims=True))
    unit = full * across * down

    def turn_columns():
        for load in loads:
            load.wait()
        columns = last_ref[...].T
        for b in range(turn_ref.shape[0] // k):
            part = slice(b * k, (b + 1) * k)
            turn_ref[part, :] = jnp.where(lane == 0, columns[:, b : b + 1], turn_ref[part, :])

    groups = inverse_rows([unit[n : n + B] for n in range(0, k, B)], k, {TURN_AT: turn_columns})
    inv_t = jnp.where(row >= lane, jnp.concatenate(groups, axis=0), 0.0) * across
    turned_inv = pltpu.roll(inv_t, 1, 1)
    left = dot(inv_t, cross, ((1,), (0,)))
    full_modes[...] = dot(turn_ref[...], turned_inv, ((1,), (1,)))
    reduced = dot(left, turned_inv, ((1,), (1,)))
    small[...] = reduced
    copies = [pltpu.make_async_copy(small, reduced_hbm, sems.at[chunks])]
    copies[0].start()
    along = jnp.sum(left * left, axis=0, keepdims=True)[:, :1]
    corner = inv_t[k - 1 : k, :]
    outside = jnp.maximum(square - along, 0.0)
    lane_row = lax.broadcasted_iota(jnp.int32, (1, k), 1)
    sums = jnp.sum(reduced * reduced, axis=0, keepdims=True)
    sums = sums + jnp.where(lane_row == k - 1, outside * corner * corner, 0.0)
    scale = lax.rsqrt(sums / row_count + 1e-06)
    size = full_modes.shape[0] // chunks
    for n in range(chunks):
        part = pl.ds(n * size, size)
        full_modes[part, :] = full_modes[part, :] * scale
        copies.append(pltpu.make_async_copy(full_modes.at[part, :], modes_hbm.at[part, :], sems.at[n]))
        copies[-1].start()
    for copy in copies:
        copy.wait()


def modes(row_count, table, s, last, chunks=4):
    rows, k = s.shape
    return pl.pallas_call(
        functools.partial(modes_kernel, row_count, chunks),
        out_shape=(
            jax.ShapeDtypeStruct((k, k), jnp.float32),
            jax.ShapeDtypeStruct(s.shape, jnp.float32),
        ),
        in_specs=[
            pl.BlockSpec(memory_space=pltpu.VMEM),
            pl.BlockSpec(memory_space=pl.ANY),
            pl.BlockSpec(memory_space=pl.ANY),
        ],
        out_specs=(pl.BlockSpec(memory_space=pl.ANY),) * 2,
        scratch_shapes=[
            pltpu.VMEM(s.shape, jnp.float32),
            pltpu.VMEM((rows // k, k), jnp.float32),
            pltpu.VMEM(s.shape, jnp.float32),
            pltpu.VMEM((k, k), jnp.float32),
            pltpu.SemaphoreType.DMA((chunks + 1,)),
            pltpu.SemaphoreType.DMA((2,)),
        ],
        compiler_params=pltpu.CompilerParams(vmem_limit_bytes=VMEM_BYTES),
        name="modes",
    )(table, s, last.reshape(rows // k, k))


AXES = ("z", "y", "c", "x")
NEAR = ("c", "x")
FAR = ("y", "z")
PIECE = 9


def count(axes):
    total = 1
    for axis in axes:
        total *= lax.axis_size(axis)
    return total


def exchange(block, axes):
    n = count(axes)
    copies = jnp.broadcast_to(block[None], (n, *block.shape))
    return lax.all_to_all(copies, axes, 0, 0, tiled=True)


def total_moments(table):
    n = count(NEAR)
    pieces = table.reshape(n, table.shape[0] // n, 1, table.shape[1])
    piece = lax.all_to_all(pieces, NEAR, 0, 0, tiled=True).sum(axis=0)
    for axis in FAR:
        piece = exchange(piece, (axis,)).sum(axis=0)
    return exchange(piece, NEAR).reshape(table.shape)


def shards(snapshots, last_snapshot):
    row_count = snapshots.shape[0] * count(AXES)
    table = moments(snapshots, last_snapshot, PIECE * count(NEAR))
    return modes(row_count, total_moments(table), snapshots, last_snapshot)


def solution(mesh):
    sizes = (12, 8, 2, 4)
    fine = Mesh(mesh.devices.reshape(sizes), AXES)
    in_specs = (P(AXES, None), P(AXES))
    out_specs = (P(), P(AXES, None))
    return jax.shard_map(shards, mesh=fine, in_specs=in_specs, out_specs=out_specs, check_vma=False)
```

```python
import functools

import jax
import jax.numpy as jnp
from jax import lax
from jax.experimental import pallas as pl
from jax.experimental.pallas import tpu as pltpu
from jax.sharding import Mesh
from jax.sharding import PartitionSpec as P

HIGHEST = lax.Precision.HIGHEST
B = 8
VMEM_BYTES = 16 * 2**20
TURN_AT = 8


def dot(left, right, dims):
    return lax.dot_general(
        left, right, (dims, ((), ())), precision=HIGHEST, preferred_element_type=jnp.float32
    )


def split(x):
    high = x.astype(jnp.bfloat16)
    rest = x - high.astype(jnp.float32)
    middle = rest.astype(jnp.bfloat16)
    return high, middle, (rest - middle.astype(jnp.float32)).astype(jnp.bfloat16)


def product(left, right):
    return lax.dot_general(
        left, right, (((1,), (0,)), ((), ())), preferred_element_type=jnp.float32
    )


def gram(s, last):
    rows, k = s.shape
    sub = lax.broadcasted_iota(jnp.int32, (16, k), 0)
    spread = jnp.concatenate([last, jnp.zeros_like(last)], axis=0)
    spread = jnp.concatenate([jnp.where(sub == b, spread, 0.0) for b in range(rows // k)], axis=1)
    high, middle, low = split(s)
    last_high, last_middle, last_low = split(spread)
    lead = jnp.concatenate([high.T, last_high], axis=0)
    first = product(lead, jnp.concatenate([high, middle], axis=1))
    second = product(lead, low)
    third = product(jnp.concatenate([middle.T, last_middle], axis=0), middle)
    fourth = product(jnp.concatenate([last_middle, last_low], axis=0), high)
    mixed = first[:k, k:] + second[:k]
    square = (mixed + mixed.T) + third[:k] + first[:k, :k]
    cross = fourth[16:] + second[k:] + third[k:] + first[k:, k:] + fourth[:16] + first[k:, :k]
    return square, jnp.sum(cross, axis=0, keepdims=True)


def moments_kernel(s_ref, last_ref, table_ref):
    k = s_ref.shape[1]
    h = k // 2
    last = last_ref[...]
    square, along = gram(s_ref[...], last)
    norm = jnp.sum(jnp.sum(last * last, axis=0, keepdims=True), axis=1, keepdims=True)
    row = lax.broadcasted_iota(jnp.int32, (h, k), 0)
    lane = lax.broadcasted_iota(jnp.int32, (h, k), 1)
    end = square[h:]
    table_ref[0:h, :] = jnp.where((lane < h) & (row > lane), pltpu.roll(end, h, 1), square[:h])
    diagonal = jnp.sum(jnp.where(row + h == lane, end, 0.0), axis=0, keepdims=True)
    diagonal = jnp.where(lane[:1] == 0, norm, diagonal)
    rest = table_ref.shape[0] - h
    sub = lax.broadcasted_iota(jnp.int32, (rest, k), 0)
    table_ref[h:, :] = jnp.where(sub == 0, along, jnp.where(sub == 1, diagonal, 0.0))


def moments(s, last, table_rows):
    rows, k = s.shape
    return pl.pallas_call(
        moments_kernel,
        out_shape=jax.ShapeDtypeStruct((table_rows, k), jnp.float32),
        name="moments",
    )(s, last.reshape(rows // k, k))


def inverse_rows(w, k, between):
    lane = lax.broadcasted_iota(jnp.int32, (B, k), 1)
    sub = lax.broadcasted_iota(jnp.int32, (B, k), 0)

    def wide(column):
        return jnp.broadcast_to(column, (B, k))

    out, w = [], list(w)
    groups = k // B
    for g in range(groups):
        if g in between:
            between[g]()
        at = g * B
        inside = (lane >= at) & (lane < at + B)
        columns = [wide(w[g][:, at + j : at + j + 1]) for j in range(B)]
        e = {(i, j): wide(columns[j][i : i + 1, :]) for j in range(B) for i in range(j + 1)}
        p = [
            jnp.where(inside, (lane == at + i).astype(jnp.float32), wide(w[g][i : i + 1, :]))
            for i in range(B)
        ]
        inner = g < groups - 1
        if inner:
            s = [wide(w[g + 1][:, at + j : at + j + 1]) for j in range(B)]
            after = jnp.where(inside, 0.0, w[g + 1])
        low, inv, pivot = {}, [None] * B, [None] * B
        for j in range(0, B, 2):
            n = j + 1
            a, b, c = e[j, j], e[j, n], e[n, n]
            ra, rd = 1.0 / a, 1.0 / (a * c - b * b)
            rs = a * rd
            inv[j], inv[n] = ra, rs
            for i in range(n, B):
                low[i, j] = e[j, i] * ra
            for m in range(j + 2, B):
                e[n, m] = e[n, m] - low[n, j] * e[j, m]
                low[m, n] = e[n, m] * rs
            pivot[j], pivot[n] = a, c - low[n, j] * b
            p[n] = p[n] - low[n, j] * p[j]
            for i in range(j + 2, B):
                for m in range(i, B):
                    e[i, m] = (e[i, m] - low[i, j] * e[j, m]) - low[i, n] * e[n, m]
                p[i] = (p[i] - low[i, j] * p[j]) - low[i, n] * p[n]
            if inner:
                s[n] = s[n] - s[j] * low[n, j]
                for m in range(j + 2, B):
                    s[m] = (s[m] - s[j] * low[m, j]) - s[n] * low[m, n]
                after = after - (s[j] * (p[j] * ra) + s[n] * (p[n] * rs))
        rows = None
        for j in range(B):
            y = p[j] * lax.rsqrt(pivot[j])
            rows = y if rows is None else jnp.where(sub == j, y, rows)
        out.append(rows)
        if not inner:
            break
        w[g + 1] = after
        if g + 2 == groups:
            continue
        q = [p[j] * inv[j] for j in range(B)]
        for j in range(B - 1, 0, -1):
            for i in range(j):
                q[i] = q[i] - low[j, i] * q[j]
        for h in range(g + 2, groups):
            t = [wide(w[h][:, at + j : at + j + 1]) * q[j] for j in range(B)]
            while len(t) > 1:
                t = [t[n] + t[n + 1] for n in range(0, len(t), 2)]
            w[h] = jnp.where(inside, 0.0, w[h]) - t[0]
    return out


def unfold(table):
    k = table.shape[1]
    h = k // 2
    row = lax.broadcasted_iota(jnp.int32, (h, k), 0)
    lane = lax.broadcasted_iota(jnp.int32, (h, k), 1)
    flip = jnp.concatenate([table, jnp.zeros((k - table.shape[0], k), jnp.float32)], axis=0).T
    head = table[:h]
    top = jnp.where((lane >= h) | (row <= lane), head, flip[:h])
    end = pltpu.roll(jnp.where(row > lane, head, flip[:h]), h, 1)
    end = jnp.where(row + h == lane, table[h + 1 : h + 2, :], end)
    bottom = jnp.where(lane < h, flip[h:], end)
    return jnp.concatenate([top, bottom], axis=0), flip[:, h : h + 1], table[h + 1 : h + 2, 0:1]


def modes_kernel(row_count, chunks, table_ref, s_ref, last_ref, reduced_hbm, modes_hbm, *scratch):
    turn_ref, full_modes, small, sems = scratch
    k = table_ref.shape[1]
    lane = lax.broadcasted_iota(jnp.int32, (k, k), 1)
    row = lax.broadcasted_iota(jnp.int32, (k, k), 0)
    full, last, square = unfold(table_ref[...])
    cross = jnp.where(lane == 0, last, full)
    diagonal = jnp.where(row == lane, full, 0.0)
    across = lax.rsqrt(jnp.sum(diagonal, axis=0, keepdims=True))
    down = lax.rsqrt(jnp.sum(diagonal, axis=1, keepdims=True))
    unit = full * across * down

    columns = last_ref[...].T

    def turn_columns(b):
        part = slice(b * k, (b + 1) * k)
        turn_ref[part, :] = jnp.where(lane == 0, columns[:, b : b + 1], s_ref[part, :])

    parts = turn_ref.shape[0] // k
    between = {TURN_AT + b: functools.partial(turn_columns, b) for b in range(parts)}
    groups = inverse_rows([unit[n : n + B] for n in range(0, k, B)], k, between)
    inv_t = jnp.where(row >= lane, jnp.concatenate(groups, axis=0), 0.0) * across
    turned_inv = pltpu.roll(inv_t, 1, 1)
    left = dot(inv_t, cross, ((1,), (0,)))
    full_modes[...] = dot(turn_ref[...], turned_inv, ((1,), (1,)))
    reduced = dot(left, turned_inv, ((1,), (1,)))
    small[...] = reduced
    copies = [pltpu.make_async_copy(small, reduced_hbm, sems.at[chunks])]
    copies[0].start()
    along = jnp.sum(left * left, axis=0, keepdims=True)[:, :1]
    corner = inv_t[k - 1 : k, :]
    outside = jnp.maximum(square - along, 0.0)
    lane_row = lax.broadcasted_iota(jnp.int32, (1, k), 1)
    sums = jnp.sum(reduced * reduced, axis=0, keepdims=True)
    sums = sums + jnp.where(lane_row == k - 1, outside * corner * corner, 0.0)
    scale = lax.rsqrt(sums / row_count + 1e-06)
    size = full_modes.shape[0] // chunks
    for n in range(chunks):
        part = pl.ds(n * size, size)
        full_modes[part, :] = full_modes[part, :] * scale
        copies.append(pltpu.make_async_copy(full_modes.at[part, :], modes_hbm.at[part, :], sems.at[n]))
        copies[-1].start()
    for copy in copies:
        copy.wait()


def modes(row_count, table, s, last, chunks=2):
    rows, k = s.shape
    return pl.pallas_call(
        functools.partial(modes_kernel, row_count, chunks),
        out_shape=(
            jax.ShapeDtypeStruct((k, k), jnp.float32),
            jax.ShapeDtypeStruct(s.shape, jnp.float32),
        ),
        in_specs=[pl.BlockSpec(memory_space=pltpu.VMEM)] * 3,
        out_specs=(pl.BlockSpec(memory_space=pl.ANY),) * 2,
        scratch_shapes=[
            pltpu.VMEM(s.shape, jnp.float32),
            pltpu.VMEM(s.shape, jnp.float32),
            pltpu.VMEM((k, k), jnp.float32),
            pltpu.SemaphoreType.DMA((chunks + 1,)),
        ],
        compiler_params=pltpu.CompilerParams(vmem_limit_bytes=VMEM_BYTES),
        name="modes",
    )(table, s, last.reshape(rows // k, k))


AXES = ("z", "y", "c", "x")
NEAR = ("y", "c")
FAR = ("z", "x")
PIECE = 5


def count(axes):
    total = 1
    for axis in axes:
        total *= lax.axis_size(axis)
    return total


def exchange(block, axes):
    n = count(axes)
    copies = jnp.broadcast_to(block[None], (n, *block.shape))
    return lax.all_to_all(copies, axes, 0, 0, tiled=True)


def total_moments(table):
    n = count(NEAR)
    pieces = table.reshape(n, table.shape[0] // n, 1, table.shape[1])
    piece = lax.all_to_all(pieces, NEAR, 0, 0, tiled=True).sum(axis=0)
    piece = exchange(piece, FAR).sum(axis=0)
    return exchange(piece, NEAR).reshape(table.shape)


def shards(snapshots, last_snapshot):
    row_count = snapshots.shape[0] * count(AXES)
    table = moments(snapshots, last_snapshot, PIECE * count(NEAR))
    return modes(row_count, total_moments(table), snapshots, last_snapshot)


def solution(mesh):
    sizes = (12, 8, 2, 4)
    fine = Mesh(mesh.devices.reshape(sizes), AXES)
    in_specs = (P(AXES, None), P(AXES))
    out_specs = (P(), P(AXES, None))
    return jax.shard_map(shards, mesh=fine, in_specs=in_specs, out_specs=out_specs, check_vma=False)
```

```python
import functools

import jax
import jax.numpy as jnp
from jax import lax
from jax.experimental import pallas as pl
from jax.experimental.pallas import tpu as pltpu
from jax.sharding import Mesh
from jax.sharding import PartitionSpec as P

HIGHEST = lax.Precision.HIGHEST
B = 8
VMEM_BYTES = 16 * 2**20
TURN_AT = 8


def dot(left, right, dims):
    return lax.dot_general(
        left, right, (dims, ((), ())), precision=HIGHEST, preferred_element_type=jnp.float32
    )


def split(x):
    high = x.astype(jnp.bfloat16)
    rest = x - high.astype(jnp.float32)
    middle = rest.astype(jnp.bfloat16)
    return high, middle, (rest - middle.astype(jnp.float32)).astype(jnp.bfloat16)


def product(left, right):
    return lax.dot_general(
        left, right, (((1,), (0,)), ((), ())), preferred_element_type=jnp.float32
    )


def gram(s, last):
    rows, k = s.shape
    sub = lax.broadcasted_iota(jnp.int32, (16, k), 0)
    spread = jnp.concatenate([last, jnp.zeros_like(last)], axis=0)
    spread = jnp.concatenate([jnp.where(sub == b, spread, 0.0) for b in range(rows // k)], axis=1)
    high, middle, low = split(s)
    last_high, last_middle, last_low = split(spread)
    lead = jnp.concatenate([high.T, last_high], axis=0)
    first = product(lead, jnp.concatenate([high, middle], axis=1))
    second = product(lead, low)
    third = product(jnp.concatenate([middle.T, last_middle], axis=0), middle)
    fourth = product(jnp.concatenate([last_middle, last_low], axis=0), high)
    mixed = first[:k, k:] + second[:k]
    square = (mixed + mixed.T) + third[:k] + first[:k, :k]
    cross = fourth[16:] + second[k:] + third[k:] + first[k:, k:] + fourth[:16] + first[k:, :k]
    return square, jnp.sum(cross, axis=0, keepdims=True)


def moments_kernel(s_ref, last_ref, table_ref):
    k = s_ref.shape[1]
    h = k // 2
    last = last_ref[...]
    square, along = gram(s_ref[...], last)
    norm = jnp.sum(jnp.sum(last * last, axis=0, keepdims=True), axis=1, keepdims=True)
    row = lax.broadcasted_iota(jnp.int32, (h, k), 0)
    lane = lax.broadcasted_iota(jnp.int32, (h, k), 1)
    end = square[h:]
    table_ref[0:h, :] = jnp.where((lane < h) & (row > lane), pltpu.roll(end, h, 1), square[:h])
    diagonal = jnp.sum(jnp.where(row + h == lane, end, 0.0), axis=0, keepdims=True)
    diagonal = jnp.where(lane[:1] == 0, norm, diagonal)
    rest = table_ref.shape[0] - h
    sub = lax.broadcasted_iota(jnp.int32, (rest, k), 0)
    table_ref[h:, :] = jnp.where(sub == 0, along, jnp.where(sub == 1, diagonal, 0.0))


def moments(s, last, table_rows):
    rows, k = s.shape
    return pl.pallas_call(
        moments_kernel,
        out_shape=jax.ShapeDtypeStruct((table_rows, k), jnp.float32),
        name="moments",
    )(s, last.reshape(rows // k, k))


def inverse_rows(w, k, between):
    lane = lax.broadcasted_iota(jnp.int32, (B, k), 1)
    sub = lax.broadcasted_iota(jnp.int32, (B, k), 0)

    def wide(column):
        return jnp.broadcast_to(column, (B, k))

    out, w = [], list(w)
    groups = k // B
    for g in range(groups):
        if g in between:
            between[g]()
        at = g * B
        inside = (lane >= at) & (lane < at + B)
        columns = [wide(w[g][:, at + j : at + j + 1]) for j in range(B)]
        e = {(i, j): wide(columns[j][i : i + 1, :]) for j in range(B) for i in range(j + 1)}
        p = [
            jnp.where(inside, (lane == at + i).astype(jnp.float32), wide(w[g][i : i + 1, :]))
            for i in range(B)
        ]
        inner = g < groups - 1
        if inner:
            s = [wide(w[g + 1][:, at + j : at + j + 1]) for j in range(B)]
            after = jnp.where(inside, 0.0, w[g + 1])
        low, inv, pivot = {}, [None] * B, [None] * B
        for j in range(0, B, 2):
            n = j + 1
            a, b, c = e[j, j], e[j, n], e[n, n]
            ra, rd = 1.0 / a, 1.0 / (a * c - b * b)
            rs = a * rd
            inv[j], inv[n] = ra, rs
            for i in range(n, B):
                low[i, j] = e[j, i] * ra
            for m in range(j + 2, B):
                e[n, m] = e[n, m] - low[n, j] * e[j, m]
                low[m, n] = e[n, m] * rs
            pivot[j], pivot[n] = a, c - low[n, j] * b
            p[n] = p[n] - low[n, j] * p[j]
            for i in range(j + 2, B):
                for m in range(i, B):
                    e[i, m] = (e[i, m] - low[i, j] * e[j, m]) - low[i, n] * e[n, m]
                p[i] = (p[i] - low[i, j] * p[j]) - low[i, n] * p[n]
            if inner:
                s[n] = s[n] - s[j] * low[n, j]
                for m in range(j + 2, B):
                    s[m] = (s[m] - s[j] * low[m, j]) - s[n] * low[m, n]
                after = after - (s[j] * (p[j] * ra) + s[n] * (p[n] * rs))
        rows = None
        for j in range(B):
            y = p[j] * lax.rsqrt(pivot[j])
            rows = y if rows is None else jnp.where(sub == j, y, rows)
        out.append(rows)
        if not inner:
            break
        w[g + 1] = after
        if g + 2 == groups:
            continue
        q = [p[j] * inv[j] for j in range(B)]
        for j in range(B - 1, 0, -1):
            for i in range(j):
                q[i] = q[i] - low[j, i] * q[j]
        for h in range(g + 2, groups):
            t = [wide(w[h][:, at + j : at + j + 1]) * q[j] for j in range(B)]
            while len(t) > 1:
                t = [t[n] + t[n + 1] for n in range(0, len(t), 2)]
            w[h] = jnp.where(inside, 0.0, w[h]) - t[0]
    return out


def unfold(table):
    k = table.shape[1]
    h = k // 2
    row = lax.broadcasted_iota(jnp.int32, (h, k), 0)
    lane = lax.broadcasted_iota(jnp.int32, (h, k), 1)
    flip = jnp.concatenate([table, jnp.zeros((k - table.shape[0], k), jnp.float32)], axis=0).T
    head = table[:h]
    top = jnp.where((lane >= h) | (row <= lane), head, flip[:h])
    end = pltpu.roll(jnp.where(row > lane, head, flip[:h]), h, 1)
    end = jnp.where(row + h == lane, table[h + 1 : h + 2, :], end)
    bottom = jnp.where(lane < h, flip[h:], end)
    return jnp.concatenate([top, bottom], axis=0), flip[:, h : h + 1], table[h + 1 : h + 2, 0:1]


def modes_kernel(row_count, chunks, table_ref, s_ref, last_ref, reduced_hbm, modes_hbm, *scratch):
    turn_ref, full_modes, small, sems = scratch
    k = table_ref.shape[1]
    lane = lax.broadcasted_iota(jnp.int32, (k, k), 1)
    row = lax.broadcasted_iota(jnp.int32, (k, k), 0)
    full, last, square = unfold(table_ref[...])
    cross = jnp.where(lane == 0, last, full)
    diagonal = jnp.where(row == lane, full, 0.0)
    across = lax.rsqrt(jnp.sum(diagonal, axis=0, keepdims=True))
    down = lax.rsqrt(jnp.sum(diagonal, axis=1, keepdims=True))
    unit = full * across * down

    columns = last_ref[...].T

    def turn_columns(b):
        part = slice(b * k, (b + 1) * k)
        turn_ref[part, :] = jnp.where(lane == 0, columns[:, b : b + 1], s_ref[part, :])

    parts = turn_ref.shape[0] // k
    between = {TURN_AT + b: functools.partial(turn_columns, b) for b in range(parts)}
    groups = inverse_rows([unit[n : n + B] for n in range(0, k, B)], k, between)
    inv_t = jnp.where(row >= lane, jnp.concatenate(groups, axis=0), 0.0) * across
    turned_inv = pltpu.roll(inv_t, 1, 1)
    left = dot(inv_t, cross, ((1,), (0,)))
    full_modes[...] = dot(turn_ref[...], turned_inv, ((1,), (1,)))
    reduced = dot(left, turned_inv, ((1,), (1,)))
    small[...] = reduced
    copies = [pltpu.make_async_copy(small, reduced_hbm, sems.at[chunks])]
    copies[0].start()
    along = jnp.sum(left * left, axis=0, keepdims=True)[:, :1]
    corner = inv_t[k - 1 : k, :]
    outside = jnp.maximum(square - along, 0.0)
    lane_row = lax.broadcasted_iota(jnp.int32, (1, k), 1)
    sums = jnp.sum(reduced * reduced, axis=0, keepdims=True)
    sums = sums + jnp.where(lane_row == k - 1, outside * corner * corner, 0.0)
    scale = lax.rsqrt(sums / row_count + 1e-06)
    size = full_modes.shape[0] // chunks
    for n in range(chunks):
        part = pl.ds(n * size, size)
        full_modes[part, :] = full_modes[part, :] * scale
        copies.append(pltpu.make_async_copy(full_modes.at[part, :], modes_hbm.at[part, :], sems.at[n]))
        copies[-1].start()
    for copy in copies:
        copy.wait()


def modes(row_count, table, s, last, chunks=2):
    rows, k = s.shape
    return pl.pallas_call(
        functools.partial(modes_kernel, row_count, chunks),
        out_shape=(
            jax.ShapeDtypeStruct((k, k), jnp.float32),
            jax.ShapeDtypeStruct(s.shape, jnp.float32),
        ),
        in_specs=[pl.BlockSpec(memory_space=pltpu.VMEM)] * 3,
        out_specs=(pl.BlockSpec(memory_space=pl.ANY),) * 2,
        scratch_shapes=[
            pltpu.VMEM(s.shape, jnp.float32),
            pltpu.VMEM(s.shape, jnp.float32),
            pltpu.VMEM((k, k), jnp.float32),
            pltpu.SemaphoreType.DMA((chunks + 1,)),
        ],
        compiler_params=pltpu.CompilerParams(vmem_limit_bytes=VMEM_BYTES),
        name="modes",
    )(table, s, last.reshape(rows // k, k))


AXES = ("zh", "zl", "y", "c", "x")
NEAR = ("zl", "c", "x")
FAR = ("zh", "y")
PIECE = 5


def count(axes):
    total = 1
    for axis in axes:
        total *= lax.axis_size(axis)
    return total


def exchange(block, axes):
    n = count(axes)
    copies = jnp.broadcast_to(block[None], (n, *block.shape))
    return lax.all_to_all(copies, axes, 0, 0, tiled=True)


def total_moments(table):
    n = count(NEAR)
    pieces = table.reshape(n, table.shape[0] // n, 1, table.shape[1])
    piece = lax.all_to_all(pieces, NEAR, 0, 0, tiled=True).sum(axis=0)
    piece = exchange(piece, FAR).sum(axis=0)
    return exchange(piece, NEAR).reshape(table.shape)


def shards(snapshots, last_snapshot):
    row_count = snapshots.shape[0] * count(AXES)
    table = moments(snapshots, last_snapshot, PIECE * count(NEAR))
    return modes(row_count, total_moments(table), snapshots, last_snapshot)


def solution(mesh):
    sizes = (6, 2, 8, 2, 4)
    fine = Mesh(mesh.devices.reshape(sizes), AXES)
    in_specs = (P(AXES, None), P(AXES))
    out_specs = (P(), P(AXES, None))
    return jax.shard_map(shards, mesh=fine, in_specs=in_specs, out_specs=out_specs, check_vma=False)
```

```python
import functools

import jax
import jax.numpy as jnp
from jax import lax
from jax.experimental import pallas as pl
from jax.experimental.pallas import tpu as pltpu
from jax.sharding import Mesh
from jax.sharding import PartitionSpec as P

HIGHEST = lax.Precision.HIGHEST
B = 8
VMEM_BYTES = 16 * 2**20
TURN_AT = 8


def dot(left, right, dims):
    return lax.dot_general(
        left, right, (dims, ((), ())), precision=HIGHEST, preferred_element_type=jnp.float32
    )


def split(x):
    high = x.astype(jnp.bfloat16)
    rest = x - high.astype(jnp.float32)
    middle = rest.astype(jnp.bfloat16)
    return high, middle, (rest - middle.astype(jnp.float32)).astype(jnp.bfloat16)


def product(left, right):
    return lax.dot_general(
        left, right, (((1,), (0,)), ((), ())), preferred_element_type=jnp.float32
    )


def gram(s, last):
    rows, k = s.shape
    sub = lax.broadcasted_iota(jnp.int32, (16, k), 0)
    spread = jnp.concatenate([last, jnp.zeros_like(last)], axis=0)
    spread = jnp.concatenate([jnp.where(sub == b, spread, 0.0) for b in range(rows // k)], axis=1)
    high, middle, low = split(s)
    last_high, last_middle, last_low = split(spread)
    lead = jnp.concatenate([high.T, last_high], axis=0)
    first = product(lead, jnp.concatenate([high, middle], axis=1))
    second = product(lead, low)
    third = product(jnp.concatenate([middle.T, last_middle], axis=0), middle)
    fourth = product(jnp.concatenate([last_middle, last_low], axis=0), high)
    mixed = first[:k, k:] + second[:k]
    square = (mixed + mixed.T) + third[:k] + first[:k, :k]
    cross = fourth[16:] + second[k:] + third[k:] + first[k:, k:] + fourth[:16] + first[k:, :k]
    return square, jnp.sum(cross, axis=0, keepdims=True)


def moments_kernel(s_ref, last_ref, table_ref):
    k = s_ref.shape[1]
    h = k // 2
    last = last_ref[...]
    square, along = gram(s_ref[...], last)
    norm = jnp.sum(jnp.sum(last * last, axis=0, keepdims=True), axis=1, keepdims=True)
    row = lax.broadcasted_iota(jnp.int32, (h, k), 0)
    lane = lax.broadcasted_iota(jnp.int32, (h, k), 1)
    end = square[h:]
    table_ref[0:h, :] = jnp.where((lane < h) & (row > lane), pltpu.roll(end, h, 1), square[:h])
    diagonal = jnp.sum(jnp.where(row + h == lane, end, 0.0), axis=0, keepdims=True)
    diagonal = jnp.where(lane[:1] == 0, norm, diagonal)
    rest = table_ref.shape[0] - h
    sub = lax.broadcasted_iota(jnp.int32, (rest, k), 0)
    table_ref[h:, :] = jnp.where(sub == 0, along, jnp.where(sub == 1, diagonal, 0.0))


def moments(s, last, table_rows):
    rows, k = s.shape
    return pl.pallas_call(
        moments_kernel,
        out_shape=jax.ShapeDtypeStruct((table_rows, k), jnp.float32),
        name="moments",
    )(s, last.reshape(rows // k, k))


def far_update(groups_of_rows, q, g, groups):
    b, k = q[0].shape
    sub = lax.broadcasted_iota(jnp.int32, (b, k), 0)
    mine = q[0]
    for j in range(1, b):
        mine = jnp.where(sub == j, q[j], mine)
    zero = jnp.zeros((b, k), jnp.float32)
    high, middle, low = split(jnp.concatenate([zero] * g + [mine] + [zero] * (groups - 1 - g), axis=0))
    left_high, left_middle, left_low = split(jnp.concatenate(groups_of_rows, axis=0))
    wide = jnp.concatenate([high, middle], axis=1)
    main = product(
        jnp.concatenate([left_high, left_middle], axis=1), jnp.concatenate([wide, wide], axis=0)
    )
    small = product(
        jnp.concatenate([left_high, left_low], axis=1), jnp.concatenate([low, high], axis=0)
    )
    return (small + main[:, k:]) + main[:, :k]


def inverse_rows(w, k, between):
    lane = lax.broadcasted_iota(jnp.int32, (B, k), 1)
    sub = lax.broadcasted_iota(jnp.int32, (B, k), 0)

    def wide(column):
        return jnp.broadcast_to(column, (B, k))

    out, w = [], list(w)
    groups = k // B
    for g in range(groups):
        if g in between:
            between[g]()
        at = g * B
        inside = (lane >= at) & (lane < at + B)
        if not g:
            columns = [wide(w[0][:, j : j + 1]) for j in range(B)]
        e = {(i, j): wide(columns[j][i : i + 1, :]) for j in range(B) for i in range(j + 1)}
        p = [
            jnp.where(inside, (lane == at + i).astype(jnp.float32), wide(w[g][i : i + 1, :]))
            for i in range(B)
        ]
        inner = g < groups - 1
        if inner:
            s = [wide(w[g + 1][:, at + j : at + j + 1]) for j in range(B)]
            after = jnp.where(inside, 0.0, w[g + 1])
            columns = [wide(w[g + 1][:, at + B + j : at + B + j + 1]) for j in range(B)]
        low, inv, pivot = {}, [None] * B, [None] * B
        for j in range(0, B, 2):
            n = j + 1
            a, b, c = e[j, j], e[j, n], e[n, n]
            ra, rd = 1.0 / a, 1.0 / (a * c - b * b)
            rs = a * rd
            inv[j], inv[n] = ra, rs
            for i in range(n, B):
                low[i, j] = e[j, i] * ra
            for m in range(j + 2, B):
                e[n, m] = e[n, m] - low[n, j] * e[j, m]
                low[m, n] = e[n, m] * rs
            pivot[j], pivot[n] = a, c - low[n, j] * b
            p[n] = p[n] - low[n, j] * p[j]
            for i in range(j + 2, B):
                for m in range(i, B):
                    e[i, m] = (e[i, m] - low[i, j] * e[j, m]) - low[i, n] * e[n, m]
                p[i] = (p[i] - low[i, j] * p[j]) - low[i, n] * p[n]
            if inner:
                s[n] = s[n] - s[j] * low[n, j]
                for m in range(j + 2, B):
                    s[m] = (s[m] - s[j] * low[m, j]) - s[n] * low[m, n]
                after = after - (s[j] * (p[j] * ra) + s[n] * (p[n] * rs))
                sj, sn = s[j] * ra, s[n] * rs
                for m in range(B):
                    both = sj * wide(s[j][m : m + 1, :]) + sn * wide(s[n][m : m + 1, :])
                    columns[m] = columns[m] - both
        rows = None
        for j in range(B):
            y = p[j] * lax.rsqrt(pivot[j])
            rows = y if rows is None else jnp.where(sub == j, y, rows)
        out.append(rows)
        if not inner:
            break
        w[g + 1] = after
        if g + 2 == groups:
            continue
        q = [p[j] * inv[j] for j in range(B)]
        for j in range(B - 1, 0, -1):
            for i in range(j):
                q[i] = q[i] - low[j, i] * q[j]
        direct = min(g + 3, groups) if groups - (g + 3) >= 2 else groups
        for h in range(g + 2, direct):
            t = [wide(w[h][:, at + j : at + j + 1]) * q[j] for j in range(B)]
            while len(t) > 1:
                t = [t[n] + t[n + 1] for n in range(0, len(t), 2)]
            w[h] = jnp.where(inside, 0.0, w[h]) - t[0]
        if direct < groups:
            rest = far_update(w[direct:], q, g, groups)
            for n, h in enumerate(range(direct, groups)):
                w[h] = jnp.where(inside, 0.0, w[h]) - rest[n * B : (n + 1) * B]
    return out


def unfold(table):
    k = table.shape[1]
    h = k // 2
    row = lax.broadcasted_iota(jnp.int32, (h, k), 0)
    lane = lax.broadcasted_iota(jnp.int32, (h, k), 1)
    flip = jnp.concatenate([table, jnp.zeros((k - table.shape[0], k), jnp.float32)], axis=0).T
    head = table[:h]
    top = jnp.where((lane >= h) | (row <= lane), head, flip[:h])
    end = pltpu.roll(jnp.where(row > lane, head, flip[:h]), h, 1)
    end = jnp.where(row + h == lane, table[h + 1 : h + 2, :], end)
    bottom = jnp.where(lane < h, flip[h:], end)
    return jnp.concatenate([top, bottom], axis=0), flip[:, h : h + 1], table[h + 1 : h + 2, 0:1]


def modes_kernel(row_count, chunks, table_ref, s_ref, last_ref, reduced_hbm, modes_hbm, *scratch):
    turn_ref, full_modes, small, sems = scratch
    k = table_ref.shape[1]
    lane = lax.broadcasted_iota(jnp.int32, (k, k), 1)
    row = lax.broadcasted_iota(jnp.int32, (k, k), 0)
    full, last, square = unfold(table_ref[...])
    cross = jnp.where(lane == 0, last, full)
    diagonal = jnp.where(row == lane, full, 0.0)
    across = lax.rsqrt(jnp.sum(diagonal, axis=0, keepdims=True))
    down = lax.rsqrt(jnp.sum(diagonal, axis=1, keepdims=True))
    unit = full * across * down

    columns = last_ref[...].T

    def turn_columns(b):
        part = slice(b * k, (b + 1) * k)
        turn_ref[part, :] = jnp.where(lane == 0, columns[:, b : b + 1], s_ref[part, :])

    parts = turn_ref.shape[0] // k
    between = {TURN_AT + b: functools.partial(turn_columns, b) for b in range(parts)}
    groups = inverse_rows([unit[n : n + B] for n in range(0, k, B)], k, between)
    inv_t = jnp.where(row >= lane, jnp.concatenate(groups, axis=0), 0.0) * across
    turned_inv = pltpu.roll(inv_t, 1, 1)
    left = dot(inv_t, cross, ((1,), (0,)))
    full_modes[...] = dot(turn_ref[...], turned_inv, ((1,), (1,)))
    reduced = dot(left, turned_inv, ((1,), (1,)))
    small[...] = reduced
    copies = [pltpu.make_async_copy(small, reduced_hbm, sems.at[chunks])]
    copies[0].start()
    along = jnp.sum(left * left, axis=0, keepdims=True)[:, :1]
    corner = inv_t[k - 1 : k, :]
    outside = jnp.maximum(square - along, 0.0)
    lane_row = lax.broadcasted_iota(jnp.int32, (1, k), 1)
    sums = jnp.sum(reduced * reduced, axis=0, keepdims=True)
    sums = sums + jnp.where(lane_row == k - 1, outside * corner * corner, 0.0)
    scale = lax.rsqrt(sums / row_count + 1e-06)
    size = full_modes.shape[0] // chunks
    for n in range(chunks):
        part = pl.ds(n * size, size)
        full_modes[part, :] = full_modes[part, :] * scale
        copies.append(pltpu.make_async_copy(full_modes.at[part, :], modes_hbm.at[part, :], sems.at[n]))
        copies[-1].start()
    for copy in copies:
        copy.wait()


def modes(row_count, table, s, last, chunks=2):
    rows, k = s.shape
    return pl.pallas_call(
        functools.partial(modes_kernel, row_count, chunks),
        out_shape=(
            jax.ShapeDtypeStruct((k, k), jnp.float32),
            jax.ShapeDtypeStruct(s.shape, jnp.float32),
        ),
        in_specs=[pl.BlockSpec(memory_space=pltpu.VMEM)] * 3,
        out_specs=(pl.BlockSpec(memory_space=pl.ANY),) * 2,
        scratch_shapes=[
            pltpu.VMEM(s.shape, jnp.float32),
            pltpu.VMEM(s.shape, jnp.float32),
            pltpu.VMEM((k, k), jnp.float32),
            pltpu.SemaphoreType.DMA((chunks + 1,)),
        ],
        compiler_params=pltpu.CompilerParams(vmem_limit_bytes=VMEM_BYTES),
        name="modes",
    )(table, s, last.reshape(rows // k, k))


AXES = ("zh", "zl", "y", "c", "x")
NEAR = ("c", "zl", "x")
FAR = ("zh", "y")
PIECE = 5


def count(axes):
    total = 1
    for axis in axes:
        total *= lax.axis_size(axis)
    return total


def exchange(block, axes):
    n = count(axes)
    copies = jnp.broadcast_to(block[None], (n, *block.shape))
    return lax.all_to_all(copies, axes, 0, 0, tiled=True)


def total_moments(table):
    n = count(NEAR)
    pieces = table.reshape(n, table.shape[0] // n, 1, table.shape[1])
    piece = lax.all_to_all(pieces, NEAR, 0, 0, tiled=True).sum(axis=0)
    piece = exchange(piece, FAR).sum(axis=0)
    return exchange(piece, NEAR).reshape(table.shape)


def shards(snapshots, last_snapshot):
    row_count = snapshots.shape[0] * count(AXES)
    table = moments(snapshots, last_snapshot, PIECE * count(NEAR))
    return modes(row_count, total_moments(table), snapshots, last_snapshot)


def solution(mesh):
    sizes = (6, 2, 8, 2, 4)
    fine = Mesh(mesh.devices.reshape(sizes), AXES)
    in_specs = (P(AXES, None), P(AXES))
    out_specs = (P(), P(AXES, None))
    return jax.shard_map(shards, mesh=fine, in_specs=in_specs, out_specs=out_specs, check_vma=False)
```

```python
import functools

import jax
import jax.numpy as jnp
from jax import lax
from jax.experimental import pallas as pl
from jax.experimental.pallas import tpu as pltpu
from jax.sharding import Mesh
from jax.sharding import PartitionSpec as P

B = 8
VMEM_BYTES = 16 * 2**20
TURN_AT = 8


def split(x):
    high = x.astype(jnp.bfloat16)
    rest = x - high.astype(jnp.float32)
    middle = rest.astype(jnp.bfloat16)
    return high, middle, (rest - middle.astype(jnp.float32)).astype(jnp.bfloat16)


def product(left, right):
    return lax.dot_general(
        left, right, (((1,), (0,)), ((), ())), preferred_element_type=jnp.float32
    )


def gram(s, last):
    rows, k = s.shape
    sub = lax.broadcasted_iota(jnp.int32, (16, k), 0)
    spread = jnp.concatenate([last, jnp.zeros_like(last)], axis=0)
    spread = jnp.concatenate([jnp.where(sub == b, spread, 0.0) for b in range(rows // k)], axis=1)
    high, middle, low = split(s)
    last_high, last_middle, last_low = split(spread)
    lead = jnp.concatenate([high.T, last_high], axis=0)
    first = product(lead, jnp.concatenate([high, middle], axis=1))
    second = product(lead, low)
    third = product(jnp.concatenate([middle.T, last_middle], axis=0), middle)
    fourth = product(jnp.concatenate([last_middle, last_low], axis=0), high)
    mixed = first[:k, k:] + second[:k]
    square = (mixed + mixed.T) + third[:k] + first[:k, :k]
    cross = fourth[16:] + second[k:] + third[k:] + first[k:, k:] + fourth[:16] + first[k:, :k]
    return square, jnp.sum(cross, axis=0, keepdims=True)


def moments_kernel(s_ref, last_ref, table_ref):
    k = s_ref.shape[1]
    h = k // 2
    last = last_ref[...]
    square, along = gram(s_ref[...], last)
    norm = jnp.sum(jnp.sum(last * last, axis=0, keepdims=True), axis=1, keepdims=True)
    row = lax.broadcasted_iota(jnp.int32, (h, k), 0)
    lane = lax.broadcasted_iota(jnp.int32, (h, k), 1)
    end = square[h:]
    table_ref[0:h, :] = jnp.where((lane < h) & (row > lane), pltpu.roll(end, h, 1), square[:h])
    diagonal = jnp.sum(jnp.where(row + h == lane, end, 0.0), axis=0, keepdims=True)
    diagonal = jnp.where(lane[:1] == 0, norm, diagonal)
    rest = table_ref.shape[0] - h
    sub = lax.broadcasted_iota(jnp.int32, (rest, k), 0)
    table_ref[h:, :] = jnp.where(sub == 0, along, jnp.where(sub == 1, diagonal, 0.0))


def moments(s, last, table_rows):
    rows, k = s.shape
    return pl.pallas_call(
        moments_kernel,
        out_shape=jax.ShapeDtypeStruct((table_rows, k), jnp.float32),
        name="moments",
    )(s, last.reshape(rows // k, k))


def far_update(groups_of_rows, q, g, groups):
    b, k = q[0].shape
    sub = lax.broadcasted_iota(jnp.int32, (b, k), 0)
    mine = q[0]
    for j in range(1, b):
        mine = jnp.where(sub == j, q[j], mine)
    zero = jnp.zeros((b, k), jnp.float32)
    high, middle, low = split(jnp.concatenate([zero] * g + [mine] + [zero] * (groups - 1 - g), axis=0))
    left_high, left_middle, left_low = split(jnp.concatenate(groups_of_rows, axis=0))
    wide = jnp.concatenate([high, middle], axis=1)
    main = product(
        jnp.concatenate([left_high, left_middle], axis=1), jnp.concatenate([wide, wide], axis=0)
    )
    small = product(
        jnp.concatenate([left_high, left_low], axis=1), jnp.concatenate([low, high], axis=0)
    )
    return (small + main[:, k:]) + main[:, :k]


def inverse_rows(w, k, between):
    lane = lax.broadcasted_iota(jnp.int32, (B, k), 1)
    sub = lax.broadcasted_iota(jnp.int32, (B, k), 0)

    def wide(column):
        return jnp.broadcast_to(column, (B, k))

    out, w = [], list(w)
    groups = k // B
    for g in range(groups):
        if g in between:
            between[g]()
        at = g * B
        inside = (lane >= at) & (lane < at + B)
        if not g:
            columns = [wide(w[0][:, j : j + 1]) for j in range(B)]
        e = {(i, j): wide(columns[j][i : i + 1, :]) for j in range(B) for i in range(j + 1)}
        p = [
            jnp.where(inside, (lane == at + i).astype(jnp.float32), wide(w[g][i : i + 1, :]))
            for i in range(B)
        ]
        inner = g < groups - 1
        if inner:
            s = [wide(w[g + 1][:, at + j : at + j + 1]) for j in range(B)]
            after = jnp.where(inside, 0.0, w[g + 1])
            columns = [wide(w[g + 1][:, at + B + j : at + B + j + 1]) for j in range(B)]
        low, inv, pivot = {}, [None] * B, [None] * B
        for j in range(0, B, 2):
            n = j + 1
            a, b, c = e[j, j], e[j, n], e[n, n]
            ra, rd = 1.0 / a, 1.0 / (a * c - b * b)
            rs = a * rd
            inv[j], inv[n] = ra, rs
            for i in range(n, B):
                low[i, j] = e[j, i] * ra
            for m in range(j + 2, B):
                e[n, m] = e[n, m] - low[n, j] * e[j, m]
                low[m, n] = e[n, m] * rs
            pivot[j], pivot[n] = a, c - low[n, j] * b
            p[n] = p[n] - low[n, j] * p[j]
            for i in range(j + 2, B):
                for m in range(i, B):
                    e[i, m] = (e[i, m] - low[i, j] * e[j, m]) - low[i, n] * e[n, m]
                p[i] = (p[i] - low[i, j] * p[j]) - low[i, n] * p[n]
            if inner:
                s[n] = s[n] - s[j] * low[n, j]
                for m in range(j + 2, B):
                    s[m] = (s[m] - s[j] * low[m, j]) - s[n] * low[m, n]
                after = after - (s[j] * (p[j] * ra) + s[n] * (p[n] * rs))
                sj, sn = s[j] * ra, s[n] * rs
                for m in range(B):
                    both = sj * wide(s[j][m : m + 1, :]) + sn * wide(s[n][m : m + 1, :])
                    columns[m] = columns[m] - both
        rows = None
        for j in range(B):
            y = p[j] * lax.rsqrt(pivot[j])
            rows = y if rows is None else jnp.where(sub == j, y, rows)
        out.append(rows)
        if not inner:
            break
        w[g + 1] = after
        if g + 2 == groups:
            continue
        q = [p[j] * inv[j] for j in range(B)]
        for j in range(B - 1, 0, -1):
            for i in range(j):
                q[i] = q[i] - low[j, i] * q[j]
        direct = min(g + 3, groups) if groups - (g + 3) >= 2 else groups
        for h in range(g + 2, direct):
            t = [wide(w[h][:, at + j : at + j + 1]) * q[j] for j in range(B)]
            while len(t) > 1:
                t = [t[n] + t[n + 1] for n in range(0, len(t), 2)]
            w[h] = jnp.where(inside, 0.0, w[h]) - t[0]
        if direct < groups:
            rest = far_update(w[direct:], q, g, groups)
            for n, h in enumerate(range(direct, groups)):
                w[h] = jnp.where(inside, 0.0, w[h]) - rest[n * B : (n + 1) * B]
    return out


def unfold(table):
    k = table.shape[1]
    h = k // 2
    row = lax.broadcasted_iota(jnp.int32, (h, k), 0)
    lane = lax.broadcasted_iota(jnp.int32, (h, k), 1)
    flip = jnp.concatenate([table, jnp.zeros((k - table.shape[0], k), jnp.float32)], axis=0).T
    head = table[:h]
    top = jnp.where((lane >= h) | (row <= lane), head, flip[:h])
    end = pltpu.roll(jnp.where(row > lane, head, flip[:h]), h, 1)
    end = jnp.where(row + h == lane, table[h + 1 : h + 2, :], end)
    bottom = jnp.where(lane < h, flip[h:], end)
    return jnp.concatenate([top, bottom], axis=0), flip[:, h : h + 1], table[h + 1 : h + 2, 0:1]


def stack(x):
    high, middle, low = split(x)
    return jnp.concatenate([high, middle], axis=1), jnp.concatenate([high, low], axis=1)


def stacked_product(lead, rest, right):
    high, middle, low = right
    k = high.shape[0]
    dims = (((1,), (1,)), ((), ()))
    twice = [jnp.concatenate([part, part], axis=1) for part in (high, middle)]
    main = lax.dot_general(
        lead, jnp.concatenate(twice, axis=0), dims, preferred_element_type=jnp.float32
    )
    small = lax.dot_general(
        rest, jnp.concatenate([low, high], axis=1), dims, preferred_element_type=jnp.float32
    )
    return (small + main[:, k:]) + main[:, :k]


def modes_kernel(row_count, chunks, table_ref, s_ref, last_ref, reduced_hbm, modes_hbm, *scratch):
    lead_ref, rest_ref, full_modes, small, sems = scratch
    k = table_ref.shape[1]
    lane = lax.broadcasted_iota(jnp.int32, (k, k), 1)
    row = lax.broadcasted_iota(jnp.int32, (k, k), 0)
    full, last, square = unfold(table_ref[...])
    crossed = split(jnp.where(lane == 0, last, full).T)
    diagonal = jnp.where(row == lane, full, 0.0)
    across = lax.rsqrt(jnp.sum(diagonal, axis=0, keepdims=True))
    down = lax.rsqrt(jnp.sum(diagonal, axis=1, keepdims=True))
    unit = full * across * down

    columns = last_ref[...].T

    def turn_columns(b):
        part = slice(b * k, (b + 1) * k)
        lead_ref[part, :], rest_ref[part, :] = stack(
            jnp.where(lane == 0, columns[:, b : b + 1], s_ref[part, :])
        )

    parts = s_ref.shape[0] // k
    between = {TURN_AT + b: functools.partial(turn_columns, b) for b in range(parts)}
    groups = inverse_rows([unit[n : n + B] for n in range(0, k, B)], k, between)
    inv_t = jnp.where(row >= lane, jnp.concatenate(groups, axis=0), 0.0) * across
    turned_inv = pltpu.roll(inv_t, 1, 1)
    left = stacked_product(*stack(inv_t), crossed)
    turned_parts = split(turned_inv)
    full_modes[...] = stacked_product(lead_ref[...], rest_ref[...], turned_parts)
    reduced = stacked_product(*stack(left), turned_parts)
    small[...] = reduced
    copies = [pltpu.make_async_copy(small, reduced_hbm, sems.at[chunks])]
    copies[0].start()
    along = jnp.sum(left * left, axis=0, keepdims=True)[:, :1]
    corner = inv_t[k - 1 : k, :]
    outside = jnp.maximum(square - along, 0.0)
    lane_row = lax.broadcasted_iota(jnp.int32, (1, k), 1)
    sums = jnp.sum(reduced * reduced, axis=0, keepdims=True)
    sums = sums + jnp.where(lane_row == k - 1, outside * corner * corner, 0.0)
    scale = lax.rsqrt(sums / row_count + 1e-06)
    size = full_modes.shape[0] // chunks
    for n in range(chunks):
        part = pl.ds(n * size, size)
        full_modes[part, :] = full_modes[part, :] * scale
        copies.append(pltpu.make_async_copy(full_modes.at[part, :], modes_hbm.at[part, :], sems.at[n]))
        copies[-1].start()
    for copy in copies:
        copy.wait()


def modes(row_count, table, s, last, chunks=2):
    rows, k = s.shape
    return pl.pallas_call(
        functools.partial(modes_kernel, row_count, chunks),
        out_shape=(
            jax.ShapeDtypeStruct((k, k), jnp.float32),
            jax.ShapeDtypeStruct(s.shape, jnp.float32),
        ),
        in_specs=[pl.BlockSpec(memory_space=pltpu.VMEM)] * 3,
        out_specs=(pl.BlockSpec(memory_space=pl.ANY),) * 2,
        scratch_shapes=[
            pltpu.VMEM((rows, 2 * k), jnp.bfloat16),
            pltpu.VMEM((rows, 2 * k), jnp.bfloat16),
            pltpu.VMEM(s.shape, jnp.float32),
            pltpu.VMEM((k, k), jnp.float32),
            pltpu.SemaphoreType.DMA((chunks + 1,)),
        ],
        compiler_params=pltpu.CompilerParams(vmem_limit_bytes=VMEM_BYTES),
        name="modes",
    )(table, s, last.reshape(rows // k, k))


AXES = ("zh", "zl", "y", "c", "x")
NEAR = ("c", "zl", "x")
FAR = ("y", "zh")
PIECE = 5


def count(axes):
    total = 1
    for axis in axes:
        total *= lax.axis_size(axis)
    return total


def exchange(block, axes):
    n = count(axes)
    copies = jnp.broadcast_to(block[None], (n, *block.shape))
    return lax.all_to_all(copies, axes, 0, 0, tiled=True)


def total_moments(table):
    n = count(NEAR)
    pieces = table.reshape(n, table.shape[0] // n, 1, table.shape[1])
    piece = lax.all_to_all(pieces, NEAR, 0, 0, tiled=True).sum(axis=0)
    piece = exchange(piece, FAR).sum(axis=0)
    return exchange(piece, NEAR).reshape(table.shape)


def shards(snapshots, last_snapshot):
    row_count = snapshots.shape[0] * count(AXES)
    table = moments(snapshots, last_snapshot, PIECE * count(NEAR))
    return modes(row_count, total_moments(table), snapshots, last_snapshot)


def solution(mesh):
    sizes = (6, 2, 8, 2, 4)
    fine = Mesh(mesh.devices.reshape(sizes), AXES)
    in_specs = (P(AXES, None), P(AXES))
    out_specs = (P(), P(AXES, None))
    return jax.shard_map(shards, mesh=fine, in_specs=in_specs, out_specs=out_specs, check_vma=False)
```

```python
import functools

import jax
import jax.numpy as jnp
from jax import lax
from jax.experimental import pallas as pl
from jax.experimental.pallas import tpu as pltpu
from jax.sharding import Mesh
from jax.sharding import PartitionSpec as P

B = 8
VMEM_BYTES = 16 * 2**20
TURN_AT = 8


def split(x):
    high = x.astype(jnp.bfloat16)
    rest = x - high.astype(jnp.float32)
    middle = rest.astype(jnp.bfloat16)
    return high, middle, (rest - middle.astype(jnp.float32)).astype(jnp.bfloat16)


def product(left, right):
    return lax.dot_general(
        left, right, (((1,), (0,)), ((), ())), preferred_element_type=jnp.float32
    )


def gram(s, last):
    rows, k = s.shape
    sub = lax.broadcasted_iota(jnp.int32, (16, k), 0)
    spread = jnp.concatenate([last, jnp.zeros_like(last)], axis=0)
    spread = jnp.concatenate([jnp.where(sub == b, spread, 0.0) for b in range(rows // k)], axis=1)
    high, middle, low = split(s)
    last_high, last_middle, last_low = split(spread)
    lead = jnp.concatenate([high.T, last_high], axis=0)
    first = product(lead, jnp.concatenate([high, middle], axis=1))
    second = product(lead, low)
    third = product(jnp.concatenate([middle.T, last_middle], axis=0), middle)
    fourth = product(jnp.concatenate([last_middle, last_low], axis=0), high)
    mixed = first[:k, k:] + second[:k]
    square = (mixed + mixed.T) + third[:k] + first[:k, :k]
    cross = fourth[16:] + second[k:] + third[k:] + first[k:, k:] + fourth[:16] + first[k:, :k]
    return square, jnp.sum(cross, axis=0, keepdims=True)


def moments_kernel(s_ref, last_ref, table_ref):
    k = s_ref.shape[1]
    h = k // 2
    last = last_ref[...]
    square, along = gram(s_ref[...], last)
    norm = jnp.sum(jnp.sum(last * last, axis=0, keepdims=True), axis=1, keepdims=True)
    row = lax.broadcasted_iota(jnp.int32, (h, k), 0)
    lane = lax.broadcasted_iota(jnp.int32, (h, k), 1)
    end = square[h:]
    table_ref[0:h, :] = jnp.where((lane < h) & (row > lane), pltpu.roll(end, h, 1), square[:h])
    diagonal = jnp.sum(jnp.where(row + h == lane, end, 0.0), axis=0, keepdims=True)
    diagonal = jnp.where(lane[:1] == 0, norm, diagonal)
    rest = table_ref.shape[0] - h
    sub = lax.broadcasted_iota(jnp.int32, (rest, k), 0)
    table_ref[h:, :] = jnp.where(sub == 0, along, jnp.where(sub == 1, diagonal, 0.0))


def moments(s, last, table_rows):
    rows, k = s.shape
    return pl.pallas_call(
        moments_kernel,
        out_shape=jax.ShapeDtypeStruct((table_rows, k), jnp.float32),
        name="moments",
    )(s, last.reshape(rows // k, k))


def far_update(groups_of_rows, q, g, groups):
    b, k = q[0].shape
    sub = lax.broadcasted_iota(jnp.int32, (b, k), 0)
    mine = q[0]
    for j in range(1, b):
        mine = jnp.where(sub == j, q[j], mine)
    zero = jnp.zeros((b, k), jnp.float32)
    high, middle, low = split(jnp.concatenate([zero] * g + [mine] + [zero] * (groups - 1 - g), axis=0))
    left_high, left_middle, left_low = split(jnp.concatenate(groups_of_rows, axis=0))
    wide = jnp.concatenate([high, middle], axis=1)
    main = product(
        jnp.concatenate([left_high, left_middle], axis=1), jnp.concatenate([wide, wide], axis=0)
    )
    small = product(
        jnp.concatenate([left_high, left_low], axis=1), jnp.concatenate([low, high], axis=0)
    )
    return (small + main[:, k:]) + main[:, :k]


def inverse_rows(w, k, between):
    lane = lax.broadcasted_iota(jnp.int32, (B, k), 1)
    sub = lax.broadcasted_iota(jnp.int32, (B, k), 0)

    def wide(column):
        return jnp.broadcast_to(column, (B, k))

    out, w = [], list(w)
    groups = k // B
    for g in range(groups):
        if g in between:
            between[g]()
        at = g * B
        inside = (lane >= at) & (lane < at + B)
        if not g:
            columns = [wide(w[0][:, j : j + 1]) for j in range(B)]
        e = {(i, j): wide(columns[j][i : i + 1, :]) for j in range(B) for i in range(j + 1)}
        p = [
            jnp.where(inside, (lane == at + i).astype(jnp.float32), wide(w[g][i : i + 1, :]))
            for i in range(B)
        ]
        inner = g < groups - 1
        if inner:
            s = ahead if g else [wide(w[1][:, j : j + 1]) for j in range(B)]
            after = jnp.where(inside, 0.0, w[g + 1])
            columns = [wide(w[g + 1][:, at + B + j : at + B + j + 1]) for j in range(B)]
        second = g + 2 < groups
        if second:
            s2 = [wide(w[g + 2][:, at + j : at + j + 1]) for j in range(B)]
            ahead = [wide(w[g + 2][:, at + B + j : at + B + j + 1]) for j in range(B)]
            after2 = jnp.where(inside, 0.0, w[g + 2])
        low, inv, pivot = {}, [None] * B, [None] * B
        for j in range(0, B, 2):
            n = j + 1
            a, b, c = e[j, j], e[j, n], e[n, n]
            ra, rd = 1.0 / a, 1.0 / (a * c - b * b)
            rs = a * rd
            inv[j], inv[n] = ra, rs
            for i in range(n, B):
                low[i, j] = e[j, i] * ra
            for m in range(j + 2, B):
                e[n, m] = e[n, m] - low[n, j] * e[j, m]
                low[m, n] = e[n, m] * rs
            pivot[j], pivot[n] = a, c - low[n, j] * b
            p[n] = p[n] - low[n, j] * p[j]
            for i in range(j + 2, B):
                for m in range(i, B):
                    e[i, m] = (e[i, m] - low[i, j] * e[j, m]) - low[i, n] * e[n, m]
                p[i] = (p[i] - low[i, j] * p[j]) - low[i, n] * p[n]
            if inner:
                s[n] = s[n] - s[j] * low[n, j]
                for m in range(j + 2, B):
                    s[m] = (s[m] - s[j] * low[m, j]) - s[n] * low[m, n]
                after = after - (s[j] * (p[j] * ra) + s[n] * (p[n] * rs))
                pj, pn = p[j] * ra, p[n] * rs
                sj, sn = s[j] * ra, s[n] * rs
                if second:
                    s2[n] = s2[n] - s2[j] * low[n, j]
                    for m in range(j + 2, B):
                        s2[m] = (s2[m] - s2[j] * low[m, j]) - s2[n] * low[m, n]
                    after2 = after2 - (s2[j] * pj + s2[n] * pn)
                    tj, tn = s2[j] * ra, s2[n] * rs
                for m in range(B):
                    first, other = wide(s[j][m : m + 1, :]), wide(s[n][m : m + 1, :])
                    columns[m] = columns[m] - (sj * first + sn * other)
                    if second:
                        ahead[m] = ahead[m] - (tj * first + tn * other)
        rows = None
        for j in range(B):
            y = p[j] * lax.rsqrt(pivot[j])
            rows = y if rows is None else jnp.where(sub == j, y, rows)
        out.append(rows)
        if not inner:
            break
        w[g + 1] = after
        if g + 2 == groups:
            continue
        q = [p[j] * inv[j] for j in range(B)]
        for j in range(B - 1, 0, -1):
            for i in range(j):
                q[i] = q[i] - low[j, i] * q[j]
        w[g + 2] = after2
        direct = g + 3
        if direct < groups:
            rest = far_update(w[direct:], q, g, groups)
            for n, h in enumerate(range(direct, groups)):
                w[h] = jnp.where(inside, 0.0, w[h]) - rest[n * B : (n + 1) * B]
    return out


def unfold(table):
    k = table.shape[1]
    h = k // 2
    row = lax.broadcasted_iota(jnp.int32, (h, k), 0)
    lane = lax.broadcasted_iota(jnp.int32, (h, k), 1)
    flip = jnp.concatenate([table, jnp.zeros((k - table.shape[0], k), jnp.float32)], axis=0).T
    head = table[:h]
    top = jnp.where((lane >= h) | (row <= lane), head, flip[:h])
    end = pltpu.roll(jnp.where(row > lane, head, flip[:h]), h, 1)
    end = jnp.where(row + h == lane, table[h + 1 : h + 2, :], end)
    bottom = jnp.where(lane < h, flip[h:], end)
    return jnp.concatenate([top, bottom], axis=0), flip[:, h : h + 1], table[h + 1 : h + 2, 0:1]


def stack(x):
    high, middle, low = split(x)
    return jnp.concatenate([high, middle], axis=1), jnp.concatenate([high, low], axis=1)


def stacked_product(lead, rest, right):
    high, middle, low = right
    k = high.shape[0]
    dims = (((1,), (1,)), ((), ()))
    twice = [jnp.concatenate([part, part], axis=1) for part in (high, middle)]
    main = lax.dot_general(
        lead, jnp.concatenate(twice, axis=0), dims, preferred_element_type=jnp.float32
    )
    small = lax.dot_general(
        rest, jnp.concatenate([low, high], axis=1), dims, preferred_element_type=jnp.float32
    )
    return (small + main[:, k:]) + main[:, :k]


def modes_kernel(row_count, chunks, table_ref, s_ref, last_ref, reduced_hbm, modes_hbm, *scratch):
    lead_ref, rest_ref, full_modes, small, sems = scratch
    k = table_ref.shape[1]
    lane = lax.broadcasted_iota(jnp.int32, (k, k), 1)
    row = lax.broadcasted_iota(jnp.int32, (k, k), 0)
    full, last, square = unfold(table_ref[...])
    crossed = split(jnp.where(lane == 0, last, full).T)
    diagonal = jnp.where(row == lane, full, 0.0)
    across = lax.rsqrt(jnp.sum(diagonal, axis=0, keepdims=True))
    down = lax.rsqrt(jnp.sum(diagonal, axis=1, keepdims=True))
    unit = full * across * down

    columns = last_ref[...].T

    def turn_columns(b):
        part = slice(b * k, (b + 1) * k)
        lead_ref[part, :], rest_ref[part, :] = stack(
            jnp.where(lane == 0, columns[:, b : b + 1], s_ref[part, :])
        )

    parts = s_ref.shape[0] // k
    between = {TURN_AT + b: functools.partial(turn_columns, b) for b in range(parts)}
    groups = inverse_rows([unit[n : n + B] for n in range(0, k, B)], k, between)
    inv_t = jnp.where(row >= lane, jnp.concatenate(groups, axis=0), 0.0) * across
    turned_inv = pltpu.roll(inv_t, 1, 1)
    left = stacked_product(*stack(inv_t), crossed)
    turned_parts = split(turned_inv)
    full_modes[...] = stacked_product(lead_ref[...], rest_ref[...], turned_parts)
    reduced = stacked_product(*stack(left), turned_parts)
    small[...] = reduced
    copies = [pltpu.make_async_copy(small, reduced_hbm, sems.at[chunks])]
    copies[0].start()
    along = jnp.sum(left * left, axis=0, keepdims=True)[:, :1]
    corner = inv_t[k - 1 : k, :]
    outside = jnp.maximum(square - along, 0.0)
    lane_row = lax.broadcasted_iota(jnp.int32, (1, k), 1)
    sums = jnp.sum(reduced * reduced, axis=0, keepdims=True)
    sums = sums + jnp.where(lane_row == k - 1, outside * corner * corner, 0.0)
    scale = lax.rsqrt(sums / row_count + 1e-06)
    size = full_modes.shape[0] // chunks
    for n in range(chunks):
        part = pl.ds(n * size, size)
        full_modes[part, :] = full_modes[part, :] * scale
        copies.append(pltpu.make_async_copy(full_modes.at[part, :], modes_hbm.at[part, :], sems.at[n]))
        copies[-1].start()
    for copy in copies:
        copy.wait()


def modes(row_count, table, s, last, chunks=4):
    rows, k = s.shape
    return pl.pallas_call(
        functools.partial(modes_kernel, row_count, chunks),
        out_shape=(
            jax.ShapeDtypeStruct((k, k), jnp.float32),
            jax.ShapeDtypeStruct(s.shape, jnp.float32),
        ),
        in_specs=[pl.BlockSpec(memory_space=pltpu.VMEM)] * 3,
        out_specs=(pl.BlockSpec(memory_space=pl.ANY),) * 2,
        scratch_shapes=[
            pltpu.VMEM((rows, 2 * k), jnp.bfloat16),
            pltpu.VMEM((rows, 2 * k), jnp.bfloat16),
            pltpu.VMEM(s.shape, jnp.float32),
            pltpu.VMEM((k, k), jnp.float32),
            pltpu.SemaphoreType.DMA((chunks + 1,)),
        ],
        compiler_params=pltpu.CompilerParams(vmem_limit_bytes=VMEM_BYTES),
        name="modes",
    )(table, s, last.reshape(rows // k, k))


AXES = ("zh", "zl", "y", "c", "x")
NEAR = ("c", "zl", "x")
FAR = ("y", "zh")
PIECE = 5


def count(axes):
    total = 1
    for axis in axes:
        total *= lax.axis_size(axis)
    return total


def exchange(block, axes):
    n = count(axes)
    copies = jnp.broadcast_to(block[None], (n, *block.shape))
    return lax.all_to_all(copies, axes, 0, 0, tiled=True)


def total_moments(table):
    n = count(NEAR)
    pieces = table.reshape(n, table.shape[0] // n, 1, table.shape[1])
    piece = lax.all_to_all(pieces, NEAR, 0, 0, tiled=True).sum(axis=0)
    piece = exchange(piece, FAR).sum(axis=0)
    return exchange(piece, NEAR).reshape(table.shape)


def shards(snapshots, last_snapshot):
    row_count = snapshots.shape[0] * count(AXES)
    table = moments(snapshots, last_snapshot, PIECE * count(NEAR))
    return modes(row_count, total_moments(table), snapshots, last_snapshot)


def solution(mesh):
    sizes = (6, 2, 8, 2, 4)
    fine = Mesh(mesh.devices.reshape(sizes), AXES)
    in_specs = (P(AXES, None), P(AXES))
    out_specs = (P(), P(AXES, None))
    return jax.shard_map(shards, mesh=fine, in_specs=in_specs, out_specs=out_specs, check_vma=False)
```
